32 devices in a mesh: ctx: 8 (over y, x, core), head: 4 (over z).
Axes of the slice: x: 2, y: 2, z: 4, core: 2. Of those that a mesh axis runs over, the one named last changes fastest.
Arguments:
- query_latent: bfloat16 [2048, 1536], P(('ctx', 'head')), may hold values from -6 to 6
- norm_gain: bfloat16 [1536], replicated, may hold values from 0.099609375 to 1.8984375
- kv_latent: bfloat16 [2048, 576], P(('ctx', 'head')), may hold values from -120 to 120
- q_up: bfloat16 [1536, 3072], P(None, 'head'), may hold values from -0.15625 to 0.15625
- absorb_key: bfloat16 [16, 128, 512], P('head'), may hold values from -0.5 to 0.5
- absorb_value: bfloat16 [16, 512, 128], P('head'), may hold values from -0.25 to 0.25
- block_owner: int32 [8], replicated, may hold values from 0 to 7, each once
Outputs:
- head_output: bfloat16 [2048, 2048], P('ctx', 'head')
The draws below stay inside these ranges and needn't reach their ends.
All inputs are finite; a program needn't handle non-finite values.
Results may differ from the reference program's by a relative error of at most 0.024.
The reference program's roundings to bfloat16 on the way (of `normed`, `q_nope`, `q_pe`, `q_abs`, `weights` and `latent_out`) count: a program that leaves them out, or rounds other values in their place, can miss the bound.
Values may be sent and summed in bfloat16 or wider, within the bound.
A program may use at most 64 MiB of HBM per device.

```python
import math
import jax
import jax.numpy as jnp
from jax import lax

QLAT = 1536
LATENT = 512
ROPE = 64
NOPE = 128
VHEAD = 128
TOK_DEV = 256
HEADS = 16
TOKENS = 2048
N_CTX = 8


def draw_kv_latent(key, part):
    row_count = TOKENS
    kv_width = LATENT + ROPE
    first_key = jax.random.fold_in(jax.random.fold_in(key, 17), 0)
    values = jax.random.normal(first_key, (row_count, kv_width), jnp.float32)
    return jnp.clip(values, -6.0, 6.0).astype(jnp.bfloat16)


def block_levels(key, shape, cuts, least, top_value):
    gain = 1.0
    for dim, parts in cuts:
        draws = jax.random.uniform(jax.random.fold_in(jax.random.fold_in(key, 6), dim), (parts,), jnp.float32, least / len(cuts), top_value / len(cuts))
        gain = gain * jnp.repeat(jnp.exp(draws), shape[dim] // parts).reshape((-1,) + (1,) * (len(shape) - 1 - dim))
    return gain


def normal_values(own_key, extent, spread, limit, pieces=(), held_as=jnp.bfloat16):
    entries = jax.random.normal(own_key, extent, jnp.float32) * spread
    if len(pieces) > 0:
        entries = block_levels(own_key, extent, pieces, -0.22, 0.18) * entries
    return jnp.clip(entries, min=-limit, max=limit).astype(held_as)


def setup_inputs(seed: int = 0) -> dict:
    key_list = jax.random.split(jax.random.key(seed), 8)
    return {
        "query_latent": normal_values(key_list[0], (TOKENS, QLAT), 1.0, 6.0, ((0, 32),)),
        "norm_gain": jnp.clip(1.0 + 0.18 * jax.random.normal(key_list[1], (QLAT,), jnp.float32), 0.099609375, 1.8984375).astype(jnp.bfloat16),
        "kv_latent": draw_kv_latent(jax.random.fold_in(key_list[7], 71), 0),
        "q_up": normal_values(key_list[3], (QLAT, HEADS * (NOPE + ROPE)), QLAT ** -0.5, 0.15625, ((1, 4),)),
        "absorb_key": normal_values(key_list[4], (HEADS, NOPE, LATENT), NOPE ** -0.5, 0.5, ((0, 4),)),
        "absorb_value": normal_values(key_list[5], (HEADS, LATENT, VHEAD), LATENT ** -0.5, 0.25, ((0, 4),)),
        "block_owner": jax.random.permutation(key_list[6], N_CTX).astype(jnp.int32),
    }


epsilon = 1e-06
masked_score = -1e+30

def row_positions(block_owner):
    row_ids = jnp.arange(TOKENS, dtype=jnp.int32)
    device = row_ids // TOK_DEV
    offset = row_ids % TOK_DEV
    half_len = TOK_DEV // 2
    ctx_ids = jnp.arange(N_CTX, dtype=jnp.int32)
    owner_ctx = lax.optimization_barrier(jnp.sum(jnp.where(device[:, None] == ctx_ids[None, :], block_owner[None, :], 0), axis=1))
    half_block = jnp.where(offset // half_len == 0, owner_ctx, 2 * N_CTX - 1 - owner_ctx)
    return (half_block * half_len + offset % half_len).astype(jnp.int32)

def rotate(values, positions):
    half_width = values.shape[-1] // 2
    frequency = jnp.exp(jnp.arange(half_width, dtype=jnp.float32) * (-math.log(10000.0) / half_width))
    angles = positions.astype(jnp.float32)[:, None, None] * frequency
    cosine = jnp.cos(angles)
    sine = jnp.sin(angles)
    front = values[..., :half_width]
    back = values[..., half_width:]
    return jnp.concatenate([front * cosine - back * sine, front * sine + back * cosine], axis=-1)

def reference(query_latent, norm_gain, kv_latent, q_up, absorb_key, absorb_value, block_owner):
    positions = row_positions(block_owner)
    query_f32 = query_latent.astype(jnp.float32)
    normed = (query_f32 * lax.rsqrt(lax.optimization_barrier(jnp.mean(query_f32 * query_f32, axis=-1, keepdims=True)) + epsilon) * norm_gain.astype(jnp.float32)).astype(jnp.bfloat16)
    projected = jnp.dot(normed, q_up, preferred_element_type=jnp.float32).reshape(TOKENS, HEADS, NOPE + ROPE)
    q_nope = projected[..., :NOPE].astype(jnp.bfloat16)
    q_pe = rotate(projected[..., NOPE:], positions).astype(jnp.bfloat16)
    q_abs = jnp.einsum('thn,hnc->thc', q_nope.astype(jnp.float32), absorb_key.astype(jnp.float32)).astype(jnp.bfloat16)
    queries = jnp.concatenate([q_abs, q_pe], axis=-1)
    blocks = queries.reshape(N_CTX, TOK_DEV, HEADS, LATENT + ROPE).transpose(0, 2, 1, 3)
    blocks = blocks.reshape(N_CTX * HEADS, TOK_DEV, LATENT + ROPE)
    block_positions = positions.reshape(N_CTX, TOK_DEV)
    score_scale = float(NOPE + ROPE) ** (-0.5)
    latent_values = kv_latent[:, :LATENT]

    def attend(flat_index):
        block_id = flat_index // HEADS
        query_rows = lax.dynamic_index_in_dim(blocks, flat_index, 0, keepdims=False)
        query_positions = lax.dynamic_index_in_dim(block_positions, block_id, 0, keepdims=False)
        scores = jnp.dot(query_rows, kv_latent.T, preferred_element_type=jnp.float32) * score_scale
        allowed = positions[None, :] <= query_positions[:, None]
        scores = jnp.where(allowed, scores, masked_score)
        row_peak = lax.optimization_barrier(jnp.max(scores, axis=-1, keepdims=True))
        weights = jnp.where(allowed, jnp.exp(scores - row_peak), 0.0)
        row_total = lax.optimization_barrier(jnp.sum(weights, axis=-1, keepdims=True))
        summed = jnp.dot(weights.astype(jnp.bfloat16), latent_values, preferred_element_type=jnp.float32)
        return (summed / row_total).astype(jnp.bfloat16)
    latent_out = lax.map(attend, jnp.arange(N_CTX * HEADS, dtype=jnp.int32))
    latent_out = latent_out.reshape(N_CTX, HEADS, TOK_DEV, LATENT).transpose(0, 2, 1, 3).reshape(TOKENS, HEADS, LATENT)
    head_output = jnp.einsum('thc,hcv->thv', latent_out.astype(jnp.float32), absorb_value.astype(jnp.float32))
    return head_output.astype(jnp.bfloat16).reshape(TOKENS, HEADS * VHEAD)
```

```python
import functools
import math

import jax
import jax.numpy as jnp
from jax import lax
from jax.experimental import pallas as pl
from jax.experimental.pallas import tpu as pltpu
from jax.sharding import PartitionSpec as P

epsilon = 1e-06
masked_score = -1e30
MESH = pl.DeviceIdType.MESH


def when(condition, action):
    if condition is True:
        action()
    else:
        pl.when(condition)(action)


def both(first, second):
    if first is True:
        return second
    if second is True:
        return first
    return jnp.logical_and(first, second)


def kernel(
    ctx_count,
    head_devices,
    owner_ref,
    query_ref,
    gain_ref,
    kv_ref,
    q_up_hbm,
    absorb_key_hbm,
    absorb_value_hbm,
    out_ref,
    q_up_ref,
    absorb_key_ref,
    absorb_value_ref,
    kv_all,
    normed_all,
    cosine_ref,
    sine_ref,
    key_pos_ref,
    projected_ref,
    queries_ref,
    kv_recv,
    kv_send,
    norm_recv,
    norm_send_up,
    norm_send_down,
    load_sem,
):
    rows = query_ref.shape[0]
    head_count, nope_width, latent_width = absorb_key_ref.shape
    value_width = absorb_value_ref.shape[2]
    head_width = q_up_ref.shape[1] // head_count
    rope_width = head_width - nope_width
    half_width = rope_width // 2
    tok_dev = rows * head_devices
    half_len = tok_dev // 2
    chips = ctx_count // 2
    bits = chips.bit_length() - 1
    last = head_devices - 1
    ctx = lax.axis_index("ctx")
    z = lax.axis_index("head")

    def across(relative):
        place = ctx
        for bit in range(bits):
            if (relative >> bit) & 1:
                weight = 2 ** (bit + 1)
                place = place + weight - 2 * weight * lax.rem(lax.div(ctx, weight), 2)
        return place

    def other_core(place):
        return place + 1 - 2 * lax.rem(place, 2)

    sibling = other_core(ctx)

    loads = [
        pltpu.make_async_copy(q_up_hbm, q_up_ref, load_sem.at[0]),
        pltpu.make_async_copy(absorb_key_hbm, absorb_key_ref, load_sem.at[1]),
        pltpu.make_async_copy(absorb_value_hbm, absorb_value_ref, load_sem.at[2]),
    ]

    barrier = pltpu.get_barrier_semaphore()
    for bit in range(bits):
        pl.semaphore_signal(barrier, inc=1, device_id=(across(1 << bit), z), device_id_type=MESH)
    pl.semaphore_signal(barrier, inc=1, device_id=(sibling, z), device_id_type=MESH)

    @pl.when(z > 0)
    def _():
        pl.semaphore_signal(barrier, inc=1, device_id=(ctx, z - 1), device_id_type=MESH)

    @pl.when(z < last)
    def _():
        pl.semaphore_signal(barrier, inc=1, device_id=(ctx, z + 1), device_id_type=MESH)

    for load in loads:
        load.start()
    kv_all[ctx * head_devices + z] = kv_ref[...]
    pl.semaphore_wait(
        barrier, bits + 1 + jnp.where(z > 0, 1, 0) + jnp.where(z < last, 1, 0)
    )

    sent = []

    def kv_copy(origin, piece, slot, target):
        index = origin * head_devices + piece
        return pltpu.make_async_remote_copy(
            src_ref=kv_all.at[index],
            dst_ref=kv_all.at[index],
            send_sem=kv_send.at[slot],
            recv_sem=kv_recv.at[index],
            device_id=target,
            device_id_type=MESH,
        )

    def send_kv(condition, origin, piece, target):
        copy = kv_copy(origin, piece, len(sent), target)
        sent.append((condition, copy))
        when(condition, copy.start)

    def wait_kv(condition, origin, piece):
        when(condition, kv_copy(origin, piece, 0, (sibling, z)).wait_recv)

    def pieces(step):
        if step == 0:
            return [(True, z, 0)]
        return [(z >= step, z - step, 1), (z + step <= last, z + step, -1)]

    def own_block(step):
        for valid, piece, way in pieces(step):
            if step > 0:
                wait_kv(valid, ctx, piece)
            if way >= 0 and step < last:
                send_kv(both(valid, z < last), ctx, piece, (ctx, z + 1))
            if way <= 0 and step < last:
                send_kv(both(valid, z > 0), ctx, piece, (ctx, z - 1))
            for bit in range(bits):
                send_kv(valid, ctx, piece, (across(1 << bit), z))
            send_kv(valid, ctx, piece, (sibling, z))

    def relay(step, relative):
        origin = across(relative)
        for valid, piece, _ in pieces(step):
            wait_kv(valid, origin, piece)
            even = lax.rem(piece + head_devices, 2) == 0
            for bit in range(bits):
                if relative < (1 << bit):
                    send_kv(both(valid, even), origin, piece, (across(1 << bit), z))
                elif relative & ((2 << bit) - 1) == 0:
                    odd = jnp.logical_not(even)
                    send_kv(both(valid, odd), origin, piece, (across(1 << bit), z))
            send_kv(valid, origin, piece, (sibling, z))

    def norm_copy(block, upward):
        send_sem, target = (
            (norm_send_up, z + 1) if upward else (norm_send_down, z - 1)
        )
        return pltpu.make_async_remote_copy(
            src_ref=normed_all.at[block],
            dst_ref=normed_all.at[block],
            send_sem=send_sem.at[block],
            recv_sem=norm_recv.at[block],
            device_id=(ctx, target),
            device_id_type=MESH,
        )

    def norm_step(step):
        @pl.when(z >= step)
        def _():
            norm_copy(z - step, True).wait_recv()

            @pl.when(z < last)
            def _():
                norm_copy(z - step, True).start()

        @pl.when(z + step <= last)
        def _():
            norm_copy(z + step, False).wait_recv()

            @pl.when(z > 0)
            def _():
                norm_copy(z + step, False).start()

    own_block(0)
    query_f32 = query_ref[...].astype(jnp.float32)
    normed_all[z] = (
        query_f32
        * lax.rsqrt(jnp.mean(query_f32 * query_f32, axis=-1, keepdims=True) + epsilon)
        * gain_ref[...].astype(jnp.float32)
    ).astype(jnp.bfloat16)

    def send_norm():
        @pl.when(z < last)
        def _():
            norm_copy(z, True).start()

        @pl.when(z > 0)
        def _():
            norm_copy(z, False).start()

    def half_base(owner, upper):
        return jnp.where(upper, 2 * ctx_count - 1 - owner, owner) * half_len

    def tables():
        own = owner_ref[ctx]
        offset = lax.broadcasted_iota(jnp.int32, (tok_dev, 1), 0)
        places = jnp.where(
            offset < half_len,
            own * half_len + offset,
            (2 * ctx_count - 1 - own) * half_len + offset - half_len,
        )
        frequency = jnp.exp(
            lax.broadcasted_iota(jnp.int32, (1, half_width), 1).astype(jnp.float32)
            * (-math.log(10000.0) / half_width)
        )
        angles = places.astype(jnp.float32) * frequency
        cosine_ref[...] = jnp.cos(angles).reshape(cosine_ref.shape)
        sine_ref[...] = jnp.sin(angles).reshape(sine_ref.shape)
        lane = lax.broadcasted_iota(jnp.int32, (1, half_len), 1)
        for index in range(ctx_count):
            owner = owner_ref[index]
            begin = index * tok_dev
            key_pos_ref[:, begin : begin + half_len] = owner * half_len + lane
            key_pos_ref[:, begin + half_len : begin + tok_dev] = (
                2 * ctx_count - 1 - owner
            ) * half_len + lane

    distances = [
        [r for r in range(chips) if bin(r).count("1") == level] for level in range(bits + 1)
    ]
    for stage in range(head_devices + bits):
        if 0 < stage < head_devices:
            own_block(stage)
        if stage == max(last - 1, 0):
            send_norm()
        for level in range(1, bits + 1):
            if 0 <= stage - level < head_devices:
                for relative in distances[level]:
                    relay(stage - level, relative)
        if stage == max(last - 1, 0):
            tables()
            for load in loads:
                load.wait()
        if stage == last and last > 0:
            norm_step(1)

    for relative in range(chips):
        for piece in range(head_devices):
            wait_kv(True, other_core(across(relative)), piece)

    factor = float(head_width) ** (-0.5) * math.log2(math.e)
    shorter = jnp.minimum(z, last - z)

    def block_body(step, carry):
        near = z + lax.div(step + 1, 2) * (1 - 2 * lax.rem(step, 2))
        far = jnp.where(z > last - z, last - step, step)
        block = jnp.where(step <= 2 * shorter, near, far)
        projected_ref[...] = jnp.dot(
            normed_all[block], q_up_ref[...], preferred_element_type=jnp.float32
        )
        cosine = cosine_ref[block]
        sine = sine_ref[block]
        for head in range(head_count):
            begin = head * head_width
            q_nope = projected_ref[:, begin : begin + nope_width].astype(jnp.bfloat16)
            q_abs = jnp.dot(q_nope, absorb_key_ref[head], preferred_element_type=jnp.float32)
            begin += nope_width
            front = projected_ref[:, begin : begin + half_width]
            back = projected_ref[:, begin + half_width : begin + rope_width]
            span = slice(head * rows, (head + 1) * rows)
            queries_ref[span, :latent_width] = q_abs.astype(jnp.bfloat16)
            queries_ref[span, latent_width:] = jnp.concatenate(
                [front * cosine - back * sine, front * sine + back * cosine], axis=-1
            ).astype(jnp.bfloat16)

        @pl.when(step + 2 <= last)
        def _():
            norm_step(step + 2)

        offset = block * rows
        base = half_base(owner_ref[ctx], offset >= half_len) + lax.rem(offset, half_len)
        query_pos = base + lax.rem(
            lax.broadcasted_iota(jnp.int32, (head_count * rows, 1), 0), rows
        )
        keys = kv_all[...].reshape(ctx_count * tok_dev, latent_width + rope_width)
        scores = lax.dot_general(
            queries_ref[...], keys, (((1,), (1,)), ((), ())), preferred_element_type=jnp.float32
        )
        scores = jnp.where(key_pos_ref[...] <= query_pos, scores, masked_score)
        peak = jnp.max(scores, axis=-1, keepdims=True)
        weights = jnp.exp2((scores - peak) * factor)
        total = jnp.sum(weights, axis=-1, keepdims=True)
        weighted = jnp.dot(
            weights.astype(jnp.bfloat16),
            keys[:, :latent_width],
            preferred_element_type=jnp.float32,
        )
        latent_out = (weighted / total).astype(jnp.bfloat16)
        for head in range(head_count):
            out_ref[block, :, head * value_width : (head + 1) * value_width] = jnp.dot(
                latent_out[head * rows : (head + 1) * rows],
                absorb_value_ref[head],
                preferred_element_type=jnp.float32,
            ).astype(jnp.bfloat16)
        return carry

    lax.fori_loop(0, head_devices, block_body, 0)

    for condition, copy in sent:
        when(condition, copy.wait_send)
    for block in range(head_devices):
        @pl.when(jnp.logical_and(z >= block, z < last))
        def _():
            norm_copy(block, True).wait_send()

        @pl.when(jnp.logical_and(z <= block, z > 0))
        def _():
            norm_copy(block, False).wait_send()


def per_device(query_latent, norm_gain, kv_latent, q_up, absorb_key, absorb_value, block_owner):
    head_devices = lax.axis_size("head")
    ctx_count = lax.axis_size("ctx")
    rows, query_width = query_latent.shape
    kv_width = kv_latent.shape[1]
    head_count, _, value_width = absorb_value.shape
    rope_half = (kv_width - absorb_key.shape[2]) // 2
    tok_dev = rows * head_devices
    piece_count = ctx_count * head_devices
    bits = (ctx_count // 2).bit_length() - 1
    slots = head_devices * ((ctx_count // 2) * (bits + 1) * 2 + 4)
    bf16, f32 = jnp.bfloat16, jnp.float32
    whole = pl.BlockSpec(memory_space=pltpu.VMEM)
    away = pl.BlockSpec(memory_space=pl.ANY)
    out = pl.pallas_call(
        functools.partial(kernel, ctx_count, head_devices),
        out_shape=jax.ShapeDtypeStruct((head_devices, rows, head_count * value_width), bf16),
        in_specs=[pl.BlockSpec(memory_space=pltpu.SMEM), whole, whole, whole, away, away, away],
        out_specs=whole,
        scratch_shapes=[
            pltpu.VMEM(q_up.shape, bf16),
            pltpu.VMEM(absorb_key.shape, bf16),
            pltpu.VMEM(absorb_value.shape, bf16),
            pltpu.VMEM((piece_count, rows, kv_width), bf16),
            pltpu.VMEM((head_devices, rows, query_width), bf16),
            pltpu.VMEM((head_devices, rows, rope_half), f32),
            pltpu.VMEM((head_devices, rows, rope_half), f32),
            pltpu.VMEM((1, ctx_count * tok_dev), jnp.int32),
            pltpu.VMEM((rows, q_up.shape[1]), f32),
            pltpu.VMEM((head_count * rows, kv_width), bf16),
            pltpu.SemaphoreType.DMA((piece_count,)),
            pltpu.SemaphoreType.DMA((slots,)),
            pltpu.SemaphoreType.DMA((head_devices,)),
            pltpu.SemaphoreType.DMA((head_devices,)),
            pltpu.SemaphoreType.DMA((head_devices,)),
            pltpu.SemaphoreType.DMA((3,)),
        ],
        compiler_params=pltpu.CompilerParams(
            collective_id=0, has_side_effects=True, vmem_limit_bytes=48 * 1024 * 1024
        ),
    )(
        block_owner,
        query_latent,
        norm_gain.reshape(1, query_width),
        kv_latent,
        q_up,
        absorb_key,
        absorb_value,
    )
    return out.reshape(tok_dev, head_count * value_width)


def solution(mesh):
    return jax.shard_map(
        per_device,
        mesh=mesh,
        in_specs=(
            P(("ctx", "head"), None),
            P(),
            P(("ctx", "head"), None),
            P(None, "head"),
            P("head", None, None),
            P("head", None, None),
            P(),
        ),
        out_specs=P("ctx", "head"),
        check_vma=False,
    )
```

```python
import functools
import math

import jax
import jax.numpy as jnp
from jax import lax
from jax.experimental import pallas as pl
from jax.experimental.pallas import tpu as pltpu
from jax.sharding import PartitionSpec as P

epsilon = 1e-06
masked_score = -1e30
MESH = pl.DeviceIdType.MESH


def when(condition, action):
    if condition is True:
        action()
    else:
        pl.when(condition)(action)


def both(first, second):
    if first is True:
        return second
    if second is True:
        return first
    return jnp.logical_and(first, second)


def kernel(
    ctx_count,
    head_devices,
    owner_ref,
    query_hbm,
    gain_hbm,
    kv_hbm,
    q_up_hbm,
    absorb_key_hbm,
    absorb_value_hbm,
    out_ref,
    query_ref,
    gain_ref,
    q_up_ref,
    absorb_key_ref,
    absorb_value_ref,
    kv_all,
    normed_all,
    cosine_ref,
    sine_ref,
    key_pos_ref,
    projected_ref,
    queries_ref,
    kv_recv,
    kv_send,
    norm_recv,
    norm_send_up,
    norm_send_down,
    load_sem,
):
    rows = query_ref.shape[0]
    head_count, nope_width, latent_width = absorb_key_ref.shape
    value_width = absorb_value_ref.shape[2]
    head_width = q_up_ref.shape[1] // head_count
    rope_width = head_width - nope_width
    half_width = rope_width // 2
    tok_dev = rows * head_devices
    half_len = tok_dev // 2
    chips = ctx_count // 2
    bits = chips.bit_length() - 1
    last = head_devices - 1
    ctx = lax.axis_index("ctx")
    z = lax.axis_index("head")

    def across(relative):
        place = ctx
        for bit in range(bits):
            if (relative >> bit) & 1:
                weight = 2 ** (bit + 1)
                place = place + weight - 2 * weight * lax.rem(lax.div(ctx, weight), 2)
        return place

    def other_core(place):
        return place + 1 - 2 * lax.rem(place, 2)

    sibling = other_core(ctx)

    halves = head_devices // 2
    half_pieces = ctx_count * halves

    def slot_of(origin, piece):
        return lax.div(piece, halves) * half_pieces + origin * halves + lax.rem(piece, halves)

    loads = [
        pltpu.make_async_copy(kv_hbm, kv_all.at[slot_of(ctx, z)], load_sem.at[3]),
        pltpu.make_async_copy(query_hbm, query_ref, load_sem.at[4]),
        pltpu.make_async_copy(gain_hbm, gain_ref, load_sem.at[5]),
        pltpu.make_async_copy(q_up_hbm, q_up_ref, load_sem.at[0]),
        pltpu.make_async_copy(absorb_key_hbm, absorb_key_ref, load_sem.at[1]),
        pltpu.make_async_copy(absorb_value_hbm, absorb_value_ref, load_sem.at[2]),
    ]

    for load in loads:
        load.start()

    barrier = pltpu.get_barrier_semaphore()
    for bit in range(bits):
        pl.semaphore_signal(barrier, inc=1, device_id=(across(1 << bit), z), device_id_type=MESH)
    pl.semaphore_signal(barrier, inc=1, device_id=(sibling, z), device_id_type=MESH)

    @pl.when(z > 0)
    def _():
        pl.semaphore_signal(barrier, inc=1, device_id=(ctx, z - 1), device_id_type=MESH)

    @pl.when(z < last)
    def _():
        pl.semaphore_signal(barrier, inc=1, device_id=(ctx, z + 1), device_id_type=MESH)

    loads[0].wait()
    pl.semaphore_wait(
        barrier, bits + 1 + jnp.where(z > 0, 1, 0) + jnp.where(z < last, 1, 0)
    )

    sent = []

    def kv_copy(origin, piece, slot, target):
        index = slot_of(origin, piece)
        return pltpu.make_async_remote_copy(
            src_ref=kv_all.at[index],
            dst_ref=kv_all.at[index],
            send_sem=kv_send.at[slot],
            recv_sem=kv_recv.at[index],
            device_id=target,
            device_id_type=MESH,
        )

    def send_kv(condition, origin, piece, target):
        copy = kv_copy(origin, piece, len(sent), target)
        sent.append((condition, copy))
        when(condition, copy.start)

    def wait_kv(condition, origin, piece):
        when(condition, kv_copy(origin, piece, 0, (sibling, z)).wait_recv)

    def pieces(step):
        if step == 0:
            return [(True, z, 0)]
        return [(z >= step, z - step, 1), (z + step <= last, z + step, -1)]

    def own_block(step):
        for valid, piece, way in pieces(step):
            if step > 0:
                wait_kv(valid, ctx, piece)
            if way >= 0 and step < last:
                send_kv(both(valid, z < last), ctx, piece, (ctx, z + 1))
            if way <= 0 and step < last:
                send_kv(both(valid, z > 0), ctx, piece, (ctx, z - 1))
            for bit in range(bits):
                send_kv(valid, ctx, piece, (across(1 << bit), z))
            send_kv(valid, ctx, piece, (sibling, z))

    def relay(step, relative):
        origin = across(relative)
        for valid, piece, _ in pieces(step):
            wait_kv(valid, origin, piece)
            even = lax.rem(piece + head_devices, 2) == 0
            for bit in range(bits):
                if relative < (1 << bit):
                    send_kv(both(valid, even), origin, piece, (across(1 << bit), z))
                elif relative & ((2 << bit) - 1) == 0:
                    odd = jnp.logical_not(even)
                    send_kv(both(valid, odd), origin, piece, (across(1 << bit), z))
            send_kv(valid, origin, piece, (sibling, z))

    def norm_copy(block, upward):
        send_sem, target = (
            (norm_send_up, z + 1) if upward else (norm_send_down, z - 1)
        )
        return pltpu.make_async_remote_copy(
            src_ref=normed_all.at[block],
            dst_ref=normed_all.at[block],
            send_sem=send_sem.at[block],
            recv_sem=norm_recv.at[block],
            device_id=(ctx, target),
            device_id_type=MESH,
        )

    def norm_step(step):
        @pl.when(z >= step)
        def _():
            norm_copy(z - step, True).wait_recv()

            @pl.when(z < last)
            def _():
                norm_copy(z - step, True).start()

        @pl.when(z + step <= last)
        def _():
            norm_copy(z + step, False).wait_recv()

            @pl.when(z > 0)
            def _():
                norm_copy(z + step, False).start()

    own_block(0)
    loads[1].wait()
    loads[2].wait()
    query_f32 = query_ref[...].astype(jnp.float32)
    normed_all[z] = (
        query_f32
        * lax.rsqrt(jnp.mean(query_f32 * query_f32, axis=-1, keepdims=True) + epsilon)
        * gain_ref[...].reshape(1, -1).astype(jnp.float32)
    ).astype(jnp.bfloat16)

    def send_norm():
        @pl.when(z < last)
        def _():
            norm_copy(z, True).start()

        @pl.when(z > 0)
        def _():
            norm_copy(z, False).start()

    def half_base(owner, upper):
        return jnp.where(upper, 2 * ctx_count - 1 - owner, owner) * half_len

    def tables():
        own = owner_ref[ctx]
        groups = 128 // half_width
        span = tok_dev // groups
        lanes = lax.broadcasted_iota(jnp.int32, (span, 128), 1)
        offset = lax.broadcasted_iota(jnp.int32, (span, 128), 0) + span * lax.div(
            lanes, half_width
        )
        places = jnp.where(
            offset < half_len,
            own * half_len + offset,
            (2 * ctx_count - 1 - own) * half_len + offset - half_len,
        )
        frequency = jnp.exp(
            lax.rem(lanes[:1], half_width).astype(jnp.float32)
            * (-math.log(10000.0) / half_width)
        )
        angles = places.astype(jnp.float32) * frequency
        cosine, sine = jnp.cos(angles), jnp.sin(angles)
        for group in range(groups):
            begin = group * half_width
            cosine_ref[group * span : (group + 1) * span] = cosine[:, begin : begin + half_width]
            sine_ref[group * span : (group + 1) * span] = sine[:, begin : begin + half_width]
        lane = lax.broadcasted_iota(jnp.int32, (1, half_len), 1)
        for index in range(ctx_count):
            owner = owner_ref[index]
            columns = slice(index * half_len, (index + 1) * half_len)
            key_pos_ref[:1, columns] = owner * half_len + lane
            key_pos_ref[1:, columns] = (2 * ctx_count - 1 - owner) * half_len + lane

    distances = [
        [r for r in range(chips) if bin(r).count("1") == level] for level in range(bits + 1)
    ]
    for stage in range(head_devices + bits):
        if 0 < stage < head_devices:
            own_block(stage)
        if stage == max(last - 1, 0):
            send_norm()
        for level in range(1, bits + 1):
            if 0 <= stage - level < head_devices:
                for relative in distances[level]:
                    relay(stage - level, relative)
        if stage == max(last - 1, 0):
            tables()
            for load in loads[3:]:
                load.wait()
        if stage == last and last > 0:
            norm_step(1)
    if last > 1:
        norm_step(2)

    for relative in range(chips):
        for piece in range(head_devices):
            wait_kv(True, other_core(across(relative)), piece)

    factor = float(head_width) ** (-0.5) * math.log2(math.e)
    shorter = jnp.minimum(z, last - z)

    def block_body(step, carry):
        near = z + lax.div(step + 1, 2) * (1 - 2 * lax.rem(step, 2))
        far = jnp.where(z > last - z, last - step, step)
        block = jnp.where(step <= 2 * shorter, near, far)
        projected_ref[...] = jnp.dot(
            normed_all[block], q_up_ref[...], preferred_element_type=jnp.float32
        )
        cosine = cosine_ref[pl.ds(pl.multiple_of(block * rows, rows), rows)]
        sine = sine_ref[pl.ds(pl.multiple_of(block * rows, rows), rows)]
        for head in range(head_count):
            begin = head * head_width
            q_nope = projected_ref[:, begin : begin + nope_width].astype(jnp.bfloat16)
            q_abs = jnp.dot(q_nope, absorb_key_ref[head], preferred_element_type=jnp.float32)
            begin += nope_width
            front = projected_ref[:, begin : begin + half_width]
            back = projected_ref[:, begin + half_width : begin + rope_width]
            span = slice(head * rows, (head + 1) * rows)
            queries_ref[span, :latent_width] = q_abs.astype(jnp.bfloat16)
            queries_ref[span, latent_width:] = jnp.concatenate(
                [front * cosine - back * sine, front * sine + back * cosine], axis=-1
            ).astype(jnp.bfloat16)

        @pl.when(jnp.logical_and(step > 0, step + 2 <= last))
        def _():
            norm_step(step + 2)

        offset = block * rows
        base = half_base(owner_ref[ctx], offset >= half_len) + lax.rem(offset, half_len)
        query_pos = base + lax.rem(
            lax.broadcasted_iota(jnp.int32, (head_count * rows, 1), 0), rows
        )

        def attend(upper):
            def rows_of(half):
                return kv_all[half * half_pieces : (half + 1) * half_pieces].reshape(
                    ctx_count * half_len, latent_width + rope_width
                )

            def score(keys):
                return lax.dot_general(
                    queries_ref[...],
                    keys,
                    (((1,), (1,)), ((), ())),
                    preferred_element_type=jnp.float32,
                )

            allowed = key_pos_ref[int(upper) : int(upper) + 1] <= query_pos
            parts = [jnp.where(allowed, score(rows_of(int(upper))), masked_score)]
            peak = jnp.max(parts[0], axis=-1, keepdims=True)
            if upper:
                parts.append(score(rows_of(0)))
                peak = jnp.maximum(peak, jnp.max(parts[1], axis=-1, keepdims=True))
            total, weighted = 0.0, 0.0
            for half, part in zip((int(upper), 0), parts):
                weights = jnp.exp2((part - peak) * factor)
                total += jnp.sum(weights, axis=-1, keepdims=True)
                weighted += jnp.dot(
                    weights.astype(jnp.bfloat16),
                    rows_of(half)[:, :latent_width],
                    preferred_element_type=jnp.float32,
                )
            queries_ref[:, :latent_width] = (weighted / total).astype(jnp.bfloat16)

        pl.when(block < halves)(functools.partial(attend, False))
        pl.when(block >= halves)(functools.partial(attend, True))
        for head in range(head_count):
            out_ref[block, :, head * value_width : (head + 1) * value_width] = jnp.dot(
                queries_ref[head * rows : (head + 1) * rows, :latent_width],
                absorb_value_ref[head],
                preferred_element_type=jnp.float32,
            ).astype(jnp.bfloat16)
        return carry

    lax.fori_loop(0, head_devices, block_body, 0)

    for condition, copy in sent:
        when(condition, copy.wait_send)
    for block in range(head_devices):
        @pl.when(jnp.logical_and(z >= block, z < last))
        def _():
            norm_copy(block, True).wait_send()

        @pl.when(jnp.logical_and(z <= block, z > 0))
        def _():
            norm_copy(block, False).wait_send()


def per_device(query_latent, norm_gain, kv_latent, q_up, absorb_key, absorb_value, block_owner):
    head_devices = lax.axis_size("head")
    ctx_count = lax.axis_size("ctx")
    rows, query_width = query_latent.shape
    kv_width = kv_latent.shape[1]
    head_count, _, value_width = absorb_value.shape
    rope_half = (kv_width - absorb_key.shape[2]) // 2
    tok_dev = rows * head_devices
    piece_count = ctx_count * head_devices
    bits = (ctx_count // 2).bit_length() - 1
    slots = head_devices * ((ctx_count // 2) * (bits + 1) * 2 + 4)
    bf16, f32 = jnp.bfloat16, jnp.float32
    whole = pl.BlockSpec(memory_space=pltpu.VMEM)
    away = pl.BlockSpec(memory_space=pl.ANY)
    out = pl.pallas_call(
        functools.partial(kernel, ctx_count, head_devices),
        out_shape=jax.ShapeDtypeStruct((head_devices, rows, head_count * value_width), bf16),
        in_specs=[pl.BlockSpec(memory_space=pltpu.SMEM)] + [away] * 6,
        out_specs=whole,
        scratch_shapes=[
            pltpu.VMEM(query_latent.shape, bf16),
            pltpu.VMEM(norm_gain.shape, bf16),
            pltpu.VMEM(q_up.shape, bf16),
            pltpu.VMEM(absorb_key.shape, bf16),
            pltpu.VMEM(absorb_value.shape, bf16),
            pltpu.VMEM((piece_count, rows, kv_width), bf16),
            pltpu.VMEM((head_devices, rows, query_width), bf16),
            pltpu.VMEM((tok_dev, rope_half), f32),
            pltpu.VMEM((tok_dev, rope_half), f32),
            pltpu.VMEM((2, ctx_count * tok_dev // 2), jnp.int32),
            pltpu.VMEM((rows, q_up.shape[1]), f32),
            pltpu.VMEM((head_count * rows, kv_width), bf16),
            pltpu.SemaphoreType.DMA((piece_count,)),
            pltpu.SemaphoreType.DMA((slots,)),
            pltpu.SemaphoreType.DMA((head_devices,)),
            pltpu.SemaphoreType.DMA((head_devices,)),
            pltpu.SemaphoreType.DMA((head_devices,)),
            pltpu.SemaphoreType.DMA((6,)),
        ],
        compiler_params=pltpu.CompilerParams(
            collective_id=0, has_side_effects=True, vmem_limit_bytes=60 * 1024 * 1024
        ),
    )(
        block_owner,
        query_latent,
        norm_gain,
        kv_latent,
        q_up,
        absorb_key,
        absorb_value,
    )
    return out.reshape(tok_dev, head_count * value_width)


def solution(mesh):
    return jax.shard_map(
        per_device,
        mesh=mesh,
        in_specs=(
            P(("ctx", "head"), None),
            P(),
            P(("ctx", "head"), None),
            P(None, "head"),
            P("head", None, None),
            P("head", None, None),
            P(),
        ),
        out_specs=P("ctx", "head"),
        check_vma=False,
    )
```

```python
import functools
import math

import jax
import jax.numpy as jnp
from jax import lax
from jax.experimental import pallas as pl
from jax.experimental.pallas import tpu as pltpu
from jax.sharding import PartitionSpec as P

epsilon = 1e-06
masked_score = -1e30
MESH = pl.DeviceIdType.MESH


def when(condition, action):
    if condition is True:
        action()
    else:
        pl.when(condition)(action)


def both(first, second):
    if first is True:
        return second
    if second is True:
        return first
    return jnp.logical_and(first, second)


def kernel(
    ctx_count,
    head_devices,
    owner_ref,
    query_hbm,
    gain_hbm,
    kv_hbm,
    q_up_hbm,
    absorb_key_hbm,
    absorb_value_hbm,
    out_ref,
    query_ref,
    gain_ref,
    q_up_ref,
    absorb_key_ref,
    absorb_value_ref,
    kv_all,
    normed_all,
    cosine_ref,
    sine_ref,
    key_pos_ref,
    projected_ref,
    queries_ref,
    kv_recv,
    kv_send,
    norm_recv,
    norm_send_up,
    norm_send_down,
    load_sem,
):
    rows = query_ref.shape[0]
    head_count, nope_width, latent_width = absorb_key_ref.shape
    value_width = absorb_value_ref.shape[2]
    head_width = q_up_ref.shape[1] // head_count
    rope_width = head_width - nope_width
    half_width = rope_width // 2
    tok_dev = rows * head_devices
    half_len = tok_dev // 2
    chips = ctx_count // 2
    bits = chips.bit_length() - 1
    last = head_devices - 1
    ctx = lax.axis_index("ctx")
    z = lax.axis_index("head")

    def across(relative):
        place = ctx
        for bit in range(bits):
            if (relative >> bit) & 1:
                weight = 2 ** (bit + 1)
                place = place + weight - 2 * weight * lax.rem(lax.div(ctx, weight), 2)
        return place

    def other_core(place):
        return place + 1 - 2 * lax.rem(place, 2)

    sibling = other_core(ctx)

    halves = head_devices // 2
    half_pieces = ctx_count * halves

    def slot_of(origin, piece):
        return lax.div(piece, halves) * half_pieces + origin * halves + lax.rem(piece, halves)

    loads = [
        pltpu.make_async_copy(kv_hbm, kv_all.at[slot_of(ctx, z)], load_sem.at[3]),
        pltpu.make_async_copy(query_hbm, query_ref, load_sem.at[4]),
        pltpu.make_async_copy(gain_hbm, gain_ref, load_sem.at[5]),
        pltpu.make_async_copy(q_up_hbm, q_up_ref, load_sem.at[0]),
        pltpu.make_async_copy(absorb_key_hbm, absorb_key_ref, load_sem.at[1]),
        pltpu.make_async_copy(absorb_value_hbm, absorb_value_ref, load_sem.at[2]),
    ]

    for load in loads:
        load.start()

    barrier = pltpu.get_barrier_semaphore()
    for bit in range(bits):
        pl.semaphore_signal(barrier, inc=1, device_id=(across(1 << bit), z), device_id_type=MESH)
    pl.semaphore_signal(barrier, inc=1, device_id=(sibling, z), device_id_type=MESH)

    kv_reach = min(3, last)
    norm_reach = min(2, last)
    partners = bits + 1
    for step in range(1, kv_reach + 1):
        for valid, place in ((z + step <= last, z + step), (z >= step, z - step)):
            partners = partners + jnp.where(valid, 1, 0)
            when(
                valid,
                functools.partial(
                    pl.semaphore_signal,
                    barrier,
                    inc=1,
                    device_id=(ctx, place),
                    device_id_type=MESH,
                ),
            )

    loads[0].wait()
    pl.semaphore_wait(barrier, partners)

    sent = []

    def kv_copy(origin, piece, slot, target):
        index = slot_of(origin, piece)
        return pltpu.make_async_remote_copy(
            src_ref=kv_all.at[index],
            dst_ref=kv_all.at[index],
            send_sem=kv_send.at[slot],
            recv_sem=kv_recv.at[index],
            device_id=target,
            device_id_type=MESH,
        )

    def send_kv(condition, origin, piece, target):
        copy = kv_copy(origin, piece, len(sent), target)
        sent.append((condition, copy))
        when(condition, copy.start)

    def wait_kv(condition, origin, piece):
        when(condition, kv_copy(origin, piece, 0, (sibling, z)).wait_recv)

    def pieces(step):
        if step == 0:
            return [(True, z, 0)]
        return [(z >= step, z - step, 1), (z + step <= last, z + step, -1)]

    def own_block(step):
        if step == 0:
            for far in range(1, kv_reach + 1):
                send_kv(z + far <= last, ctx, z, (ctx, z + far))
                send_kv(z >= far, ctx, z, (ctx, z - far))
        for valid, piece, way in pieces(step):
            if step > 0:
                wait_kv(valid, ctx, piece)
            if kv_reach <= step < last:
                onward = z < last if way > 0 else z > 0
                send_kv(both(valid, onward), ctx, piece, (ctx, z + way))
            for bit in range(bits):
                send_kv(valid, ctx, piece, (across(1 << bit), z))
            send_kv(valid, ctx, piece, (sibling, z))

    def relay(step, relative):
        origin = across(relative)
        for valid, piece, _ in pieces(step):
            wait_kv(valid, origin, piece)
            even = lax.rem(piece + head_devices, 2) == 0
            for bit in range(bits):
                if relative < (1 << bit):
                    send_kv(both(valid, even), origin, piece, (across(1 << bit), z))
                elif relative & ((2 << bit) - 1) == 0:
                    odd = jnp.logical_not(even)
                    send_kv(both(valid, odd), origin, piece, (across(1 << bit), z))
            send_kv(valid, origin, piece, (sibling, z))

    def norm_copy(block, way, far=1):
        send_sem = norm_send_up if way > 0 else norm_send_down
        return pltpu.make_async_remote_copy(
            src_ref=normed_all.at[block],
            dst_ref=normed_all.at[block],
            send_sem=send_sem.at[block if far == 1 else last + far],
            recv_sem=norm_recv.at[block],
            device_id=(ctx, z + far * way),
            device_id_type=MESH,
        )

    def norm_step(step):
        for valid, block, way, onward in (
            (z >= step, z - step, 1, z < last),
            (z + step <= last, z + step, -1, z > 0),
        ):
            copy = norm_copy(block, way)
            when(valid, copy.wait_recv)
            when(both(valid, jnp.logical_and(onward, step >= norm_reach)), copy.start)

    own_block(0)
    loads[1].wait()
    loads[2].wait()
    query_f32 = query_ref[...].astype(jnp.float32)
    normed_all[z] = (
        query_f32
        * lax.rsqrt(jnp.mean(query_f32 * query_f32, axis=-1, keepdims=True) + epsilon)
        * gain_ref[...].reshape(1, -1).astype(jnp.float32)
    ).astype(jnp.bfloat16)

    for far in range(1, norm_reach + 1):
        when(z + far <= last, norm_copy(z, 1, far).start)
        when(z >= far, norm_copy(z, -1, far).start)

    def half_base(owner, upper):
        return jnp.where(upper, 2 * ctx_count - 1 - owner, owner) * half_len

    def tables():
        own = owner_ref[ctx]
        groups = 128 // half_width
        span = tok_dev // groups
        lanes = lax.broadcasted_iota(jnp.int32, (span, 128), 1)
        offset = lax.broadcasted_iota(jnp.int32, (span, 128), 0) + span * lax.div(
            lanes, half_width
        )
        places = jnp.where(
            offset < half_len,
            own * half_len + offset,
            (2 * ctx_count - 1 - own) * half_len + offset - half_len,
        )
        frequency = jnp.exp(
            lax.rem(lanes[:1], half_width).astype(jnp.float32)
            * (-math.log(10000.0) / half_width)
        )
        angles = places.astype(jnp.float32) * frequency
        cosine, sine = jnp.cos(angles), jnp.sin(angles)
        for group in range(groups):
            begin = group * half_width
            cosine_ref[group * span : (group + 1) * span] = cosine[:, begin : begin + half_width]
            sine_ref[group * span : (group + 1) * span] = sine[:, begin : begin + half_width]
        lane = lax.broadcasted_iota(jnp.int32, (1, half_len), 1)
        for index in range(ctx_count):
            owner = owner_ref[index]
            columns = slice(index * half_len, (index + 1) * half_len)
            key_pos_ref[:1, columns] = owner * half_len + lane
            key_pos_ref[1:, columns] = (2 * ctx_count - 1 - owner) * half_len + lane

    distances = [
        [r for r in range(chips) if bin(r).count("1") == level] for level in range(bits + 1)
    ]
    for stage in range(head_devices + bits):
        if 0 < stage < head_devices:
            own_block(stage)
        for level in range(1, bits + 1):
            if 0 <= stage - level < head_devices:
                for relative in distances[level]:
                    relay(stage - level, relative)
        if stage == 0:
            tables()
    for step in range(1, norm_reach + 1):
        norm_step(step)
    for load in loads[3:]:
        load.wait()

    factor = float(head_width) ** (-0.5) * math.log2(math.e)
    shorter = jnp.minimum(z, last - z)

    def block_at(step):
        near = z + lax.div(step + 1, 2) * (1 - 2 * lax.rem(step, 2))
        far = jnp.where(z > last - z, last - step, step)
        return jnp.where(step <= 2 * shorter, near, far)

    def project(block):
        projected_ref[...] = jnp.dot(
            normed_all[block], q_up_ref[...], preferred_element_type=jnp.float32
        )
        cosine = cosine_ref[pl.ds(pl.multiple_of(block * rows, rows), rows)]
        sine = sine_ref[pl.ds(pl.multiple_of(block * rows, rows), rows)]
        for head in range(head_count):
            begin = head * head_width
            q_nope = projected_ref[:, begin : begin + nope_width].astype(jnp.bfloat16)
            q_abs = jnp.dot(q_nope, absorb_key_ref[head], preferred_element_type=jnp.float32)
            begin += nope_width
            front = projected_ref[:, begin : begin + half_width]
            back = projected_ref[:, begin + half_width : begin + rope_width]
            span = slice(head * rows, (head + 1) * rows)
            queries_ref[span, :latent_width] = q_abs.astype(jnp.bfloat16)
            queries_ref[span, latent_width:] = jnp.concatenate(
                [front * cosine - back * sine, front * sine + back * cosine], axis=-1
            ).astype(jnp.bfloat16)

    project(z)
    for relative in range(chips):
        for piece in range(head_devices):
            wait_kv(True, other_core(across(relative)), piece)

    def block_body(step, carry):
        block = block_at(step)
        offset = block * rows
        base = half_base(owner_ref[ctx], offset >= half_len) + lax.rem(offset, half_len)
        query_pos = base + lax.rem(
            lax.broadcasted_iota(jnp.int32, (head_count * rows, 1), 0), rows
        )

        def attend(upper):
            def rows_of(half):
                return kv_all[half * half_pieces : (half + 1) * half_pieces].reshape(
                    ctx_count * half_len, latent_width + rope_width
                )

            def score(keys):
                return lax.dot_general(
                    queries_ref[...],
                    keys,
                    (((1,), (1,)), ((), ())),
                    preferred_element_type=jnp.float32,
                )

            allowed = key_pos_ref[int(upper) : int(upper) + 1] <= query_pos
            parts = [jnp.where(allowed, score(rows_of(int(upper))), masked_score)]
            peak = jnp.max(parts[0], axis=-1, keepdims=True)
            if upper:
                parts.append(score(rows_of(0)))
                peak = jnp.maximum(peak, jnp.max(parts[1], axis=-1, keepdims=True))
            total, weighted = 0.0, 0.0
            for half, part in zip((int(upper), 0), parts):
                weights = jnp.exp2((part - peak) * factor)
                total += jnp.sum(weights, axis=-1, keepdims=True)
                weighted += jnp.dot(
                    weights.astype(jnp.bfloat16),
                    rows_of(half)[:, :latent_width],
                    preferred_element_type=jnp.float32,
                )
            queries_ref[:, :latent_width] = (weighted / total).astype(jnp.bfloat16)

        pl.when(block < halves)(functools.partial(attend, False))
        pl.when(block >= halves)(functools.partial(attend, True))
        for head in range(head_count):
            out_ref[block, :, head * value_width : (head + 1) * value_width] = jnp.dot(
                queries_ref[head * rows : (head + 1) * rows, :latent_width],
                absorb_value_ref[head],
                preferred_element_type=jnp.float32,
            ).astype(jnp.bfloat16)

        @pl.when(step < last)
        def _():
            @pl.when(step + 1 > norm_reach)
            def _():
                norm_step(step + 1)

            project(block_at(step + 1))

        return carry

    lax.fori_loop(0, head_devices, block_body, 0)

    for condition, copy in sent:
        when(condition, copy.wait_send)
    for far in range(1, norm_reach + 1):
        when(z + far <= last, norm_copy(z, 1, far).wait_send)
        when(z >= far, norm_copy(z, -1, far).wait_send)
    for step in range(norm_reach, last):
        when(both(z >= step, z < last), norm_copy(z - step, 1).wait_send)
        when(both(z + step <= last, z > 0), norm_copy(z + step, -1).wait_send)


def per_device(query_latent, norm_gain, kv_latent, q_up, absorb_key, absorb_value, block_owner):
    head_devices = lax.axis_size("head")
    ctx_count = lax.axis_size("ctx")
    rows, query_width = query_latent.shape
    kv_width = kv_latent.shape[1]
    head_count, _, value_width = absorb_value.shape
    rope_half = (kv_width - absorb_key.shape[2]) // 2
    tok_dev = rows * head_devices
    piece_count = ctx_count * head_devices
    bits = (ctx_count // 2).bit_length() - 1
    slots = head_devices * ((ctx_count // 2) * (bits + 1) * 2 + 8)
    bf16, f32 = jnp.bfloat16, jnp.float32
    whole = pl.BlockSpec(memory_space=pltpu.VMEM)
    away = pl.BlockSpec(memory_space=pl.ANY)
    out = pl.pallas_call(
        functools.partial(kernel, ctx_count, head_devices),
        out_shape=jax.ShapeDtypeStruct((head_devices, rows, head_count * value_width), bf16),
        in_specs=[pl.BlockSpec(memory_space=pltpu.SMEM)] + [away] * 6,
        out_specs=whole,
        scratch_shapes=[
            pltpu.VMEM(query_latent.shape, bf16),
            pltpu.VMEM(norm_gain.shape, bf16),
            pltpu.VMEM(q_up.shape, bf16),
            pltpu.VMEM(absorb_key.shape, bf16),
            pltpu.VMEM(absorb_value.shape, bf16),
            pltpu.VMEM((piece_count, rows, kv_width), bf16),
            pltpu.VMEM((head_devices, rows, query_width), bf16),
            pltpu.VMEM((tok_dev, rope_half), f32),
            pltpu.VMEM((tok_dev, rope_half), f32),
            pltpu.VMEM((2, ctx_count * tok_dev // 2), jnp.int32),
            pltpu.VMEM((rows, q_up.shape[1]), f32),
            pltpu.VMEM((head_count * rows, kv_width), bf16),
            pltpu.SemaphoreType.DMA((piece_count,)),
            pltpu.SemaphoreType.DMA((slots,)),
            pltpu.SemaphoreType.DMA((head_devices,)),
            pltpu.SemaphoreType.DMA((head_devices + 2,)),
            pltpu.SemaphoreType.DMA((head_devices + 2,)),
            pltpu.SemaphoreType.DMA((6,)),
        ],
        compiler_params=pltpu.CompilerParams(
            collective_id=0, has_side_effects=True, vmem_limit_bytes=60 * 1024 * 1024
        ),
    )(
        block_owner,
        query_latent,
        norm_gain,
        kv_latent,
        q_up,
        absorb_key,
        absorb_value,
    )
    return out.reshape(tok_dev, head_count * value_width)


def solution(mesh):
    return jax.shard_map(
        per_device,
        mesh=mesh,
        in_specs=(
            P(("ctx", "head"), None),
            P(),
            P(("ctx", "head"), None),
            P(None, "head"),
            P("head", None, None),
            P("head", None, None),
            P(),
        ),
        out_specs=P("ctx", "head"),
        check_vma=False,
    )
```

```python
import functools
import math

import jax
import jax.numpy as jnp
from jax import lax
from jax.experimental import pallas as pl
from jax.experimental.pallas import tpu as pltpu
from jax.sharding import PartitionSpec as P

epsilon = 1e-06
masked_score = -1e30
MESH = pl.DeviceIdType.MESH


def when(condition, action):
    if condition is True:
        action()
    else:
        pl.when(condition)(action)


def both(first, second):
    if first is True:
        return second
    if second is True:
        return first
    return jnp.logical_and(first, second)


def kernel(
    ctx_count,
    head_devices,
    owner_ref,
    query_hbm,
    gain_hbm,
    kv_hbm,
    q_up_hbm,
    absorb_key_hbm,
    absorb_value_hbm,
    out_ref,
    kv_ref,
    query_ref,
    gain_ref,
    q_up_ref,
    absorb_key_ref,
    absorb_value_ref,
    kv_all,
    normed_all,
    cosine_ref,
    sine_ref,
    key_pos_ref,
    projected_ref,
    queries_ref,
    kv_recv,
    kv_send,
    norm_recv,
    norm_send_up,
    norm_send_down,
    load_sem,
):
    rows = query_ref.shape[0]
    head_count, nope_width, latent_width = absorb_key_ref.shape
    value_width = absorb_value_ref.shape[2]
    head_width = q_up_ref.shape[1] // head_count
    rope_width = head_width - nope_width
    half_width = rope_width // 2
    tok_dev = rows * head_devices
    half_len = tok_dev // 2
    chips = ctx_count // 2
    bits = chips.bit_length() - 1
    last = head_devices - 1
    ctx = lax.axis_index("ctx")
    z = lax.axis_index("head")

    def across(relative):
        place = ctx
        for bit in range(bits):
            if (relative >> bit) & 1:
                weight = 2 ** (bit + 1)
                place = place + weight - 2 * weight * lax.rem(lax.div(ctx, weight), 2)
        return place

    def other_core(place):
        return place + 1 - 2 * lax.rem(place, 2)

    sibling = other_core(ctx)

    halves = head_devices // 2
    half_pieces = ctx_count * halves

    def slot_of(origin, piece):
        return lax.div(piece, halves) * half_pieces + origin * halves + lax.rem(piece, halves)

    loads = [
        pltpu.make_async_copy(kv_hbm, kv_ref, load_sem.at[3]),
        pltpu.make_async_copy(query_hbm, query_ref, load_sem.at[4]),
        pltpu.make_async_copy(gain_hbm, gain_ref, load_sem.at[5]),
        pltpu.make_async_copy(q_up_hbm, q_up_ref, load_sem.at[0]),
        pltpu.make_async_copy(absorb_key_hbm, absorb_key_ref, load_sem.at[1]),
        pltpu.make_async_copy(absorb_value_hbm, absorb_value_ref, load_sem.at[2]),
    ]

    for load in loads:
        load.start()

    barrier = pltpu.get_barrier_semaphore()
    for bit in range(bits):
        pl.semaphore_signal(barrier, inc=1, device_id=(across(1 << bit), z), device_id_type=MESH)
    pl.semaphore_signal(barrier, inc=1, device_id=(sibling, z), device_id_type=MESH)

    kv_reach = min(3, last)
    norm_reach = min(2, last)
    partners = bits + 1
    for step in range(1, kv_reach + 1):
        for valid, place in ((z + step <= last, z + step), (z >= step, z - step)):
            partners = partners + jnp.where(valid, 1, 0)
            when(
                valid,
                functools.partial(
                    pl.semaphore_signal,
                    barrier,
                    inc=1,
                    device_id=(ctx, place),
                    device_id_type=MESH,
                ),
            )

    loads[0].wait()
    kv_width = latent_width + rope_width
    own_slot = slot_of(ctx, z)
    kv_all[own_slot, :, :kv_width] = kv_ref[...]
    padding = kv_all.shape[2] - kv_width
    if padding:
        kv_all[own_slot, :, kv_width:] = jnp.zeros((rows, padding), jnp.bfloat16)
        queries_ref[:, kv_width:] = jnp.zeros((head_count * rows, padding), jnp.bfloat16)
    pl.semaphore_wait(barrier, partners)

    sent = []

    def kv_copy(origin, piece, slot, target):
        index = slot_of(origin, piece)
        return pltpu.make_async_remote_copy(
            src_ref=kv_all.at[index],
            dst_ref=kv_all.at[index],
            send_sem=kv_send.at[slot],
            recv_sem=kv_recv.at[index],
            device_id=target,
            device_id_type=MESH,
        )

    def send_kv(condition, origin, piece, target):
        copy = kv_copy(origin, piece, len(sent), target)
        sent.append((condition, copy))
        when(condition, copy.start)

    def wait_kv(condition, origin, piece):
        when(condition, kv_copy(origin, piece, 0, (sibling, z)).wait_recv)

    def pieces(step):
        if step == 0:
            return [(True, z, 0)]
        return [(z >= step, z - step, 1), (z + step <= last, z + step, -1)]

    def own_block(step):
        if step == 0:
            for far in range(1, kv_reach + 1):
                send_kv(z + far <= last, ctx, z, (ctx, z + far))
                send_kv(z >= far, ctx, z, (ctx, z - far))
        for valid, piece, way in pieces(step):
            if step > 0:
                wait_kv(valid, ctx, piece)
            if kv_reach <= step < last:
                onward = z < last if way > 0 else z > 0
                send_kv(both(valid, onward), ctx, piece, (ctx, z + way))
            for bit in range(bits):
                send_kv(valid, ctx, piece, (across(1 << bit), z))
            send_kv(valid, ctx, piece, (sibling, z))

    def relay(step, relative):
        origin = across(relative)
        for valid, piece, _ in pieces(step):
            wait_kv(valid, origin, piece)
            even = lax.rem(piece + head_devices, 2) == 0
            for bit in range(bits):
                if relative < (1 << bit):
                    send_kv(both(valid, even), origin, piece, (across(1 << bit), z))
                elif relative & ((2 << bit) - 1) == 0:
                    odd = jnp.logical_not(even)
                    send_kv(both(valid, odd), origin, piece, (across(1 << bit), z))
            send_kv(valid, origin, piece, (sibling, z))

    def norm_copy(block, way, far=1):
        send_sem = norm_send_up if way > 0 else norm_send_down
        return pltpu.make_async_remote_copy(
            src_ref=normed_all.at[block],
            dst_ref=normed_all.at[block],
            send_sem=send_sem.at[block if far == 1 else last + far],
            recv_sem=norm_recv.at[block],
            device_id=(ctx, z + far * way),
            device_id_type=MESH,
        )

    def norm_step(step):
        for valid, block, way, onward in (
            (z >= step, z - step, 1, z < last),
            (z + step <= last, z + step, -1, z > 0),
        ):
            copy = norm_copy(block, way)
            when(valid, copy.wait_recv)
            when(both(valid, jnp.logical_and(onward, step >= norm_reach)), copy.start)

    own_block(0)
    loads[1].wait()
    loads[2].wait()
    query_f32 = query_ref[...].astype(jnp.float32)
    normed_all[z] = (
        query_f32
        * lax.rsqrt(jnp.mean(query_f32 * query_f32, axis=-1, keepdims=True) + epsilon)
        * gain_ref[...].reshape(1, -1).astype(jnp.float32)
    ).astype(jnp.bfloat16)

    for far in range(1, norm_reach + 1):
        when(z + far <= last, norm_copy(z, 1, far).start)
        when(z >= far, norm_copy(z, -1, far).start)

    def half_base(owner, upper):
        return jnp.where(upper, 2 * ctx_count - 1 - owner, owner) * half_len

    def tables():
        own = owner_ref[ctx]
        groups = 128 // half_width
        span = tok_dev // groups
        lanes = lax.broadcasted_iota(jnp.int32, (span, 128), 1)
        offset = lax.broadcasted_iota(jnp.int32, (span, 128), 0) + span * lax.div(
            lanes, half_width
        )
        places = jnp.where(
            offset < half_len,
            own * half_len + offset,
            (2 * ctx_count - 1 - own) * half_len + offset - half_len,
        )
        frequency = jnp.exp(
            lax.rem(lanes[:1], half_width).astype(jnp.float32)
            * (-math.log(10000.0) / half_width)
        )
        angles = places.astype(jnp.float32) * frequency
        cosine, sine = jnp.cos(angles), jnp.sin(angles)
        for group in range(groups):
            begin = group * half_width
            cosine_ref[group * span : (group + 1) * span] = cosine[:, begin : begin + half_width]
            sine_ref[group * span : (group + 1) * span] = sine[:, begin : begin + half_width]
        lane = lax.broadcasted_iota(jnp.int32, (1, half_len), 1)
        for index in range(ctx_count):
            owner = owner_ref[index]
            columns = slice(index * half_len, (index + 1) * half_len)
            key_pos_ref[:1, columns] = owner * half_len + lane
            key_pos_ref[1:, columns] = (2 * ctx_count - 1 - owner) * half_len + lane

    distances = [
        [r for r in range(chips) if bin(r).count("1") == level] for level in range(bits + 1)
    ]
    for stage in range(head_devices + bits):
        if 0 < stage < head_devices:
            own_block(stage)
        for level in range(1, bits + 1):
            if 0 <= stage - level < head_devices:
                for relative in distances[level]:
                    relay(stage - level, relative)
        if stage == 0:
            tables()
    for step in range(1, norm_reach + 1):
        norm_step(step)
    for load in loads[3:]:
        load.wait()

    factor = float(head_width) ** (-0.5) * math.log2(math.e)
    shorter = jnp.minimum(z, last - z)

    def block_at(step):
        near = z + lax.div(step + 1, 2) * (1 - 2 * lax.rem(step, 2))
        far = jnp.where(z > last - z, last - step, step)
        return jnp.where(step <= 2 * shorter, near, far)

    def project(block):
        projected_ref[...] = jnp.dot(
            normed_all[block], q_up_ref[...], preferred_element_type=jnp.float32
        )
        cosine = cosine_ref[pl.ds(pl.multiple_of(block * rows, rows), rows)]
        sine = sine_ref[pl.ds(pl.multiple_of(block * rows, rows), rows)]
        for head in range(head_count):
            begin = head * head_width
            q_nope = projected_ref[:, begin : begin + nope_width].astype(jnp.bfloat16)
            q_abs = jnp.dot(q_nope, absorb_key_ref[head], preferred_element_type=jnp.float32)
            begin += nope_width
            front = projected_ref[:, begin : begin + half_width]
            back = projected_ref[:, begin + half_width : begin + rope_width]
            span = slice(head * rows, (head + 1) * rows)
            queries_ref[span, :latent_width] = q_abs.astype(jnp.bfloat16)
            queries_ref[span, latent_width:kv_width] = jnp.concatenate(
                [front * cosine - back * sine, front * sine + back * cosine], axis=-1
            ).astype(jnp.bfloat16)

    project(z)
    for relative in range(chips):
        for piece in range(head_devices):
            wait_kv(True, other_core(across(relative)), piece)

    def block_body(step, carry):
        block = block_at(step)
        offset = block * rows
        base = half_base(owner_ref[ctx], offset >= half_len) + lax.rem(offset, half_len)
        query_pos = base + lax.rem(
            lax.broadcasted_iota(jnp.int32, (head_count * rows, 1), 0), rows
        )

        def attend(upper):
            def rows_of(half):
                return kv_all[half * half_pieces : (half + 1) * half_pieces].reshape(
                    ctx_count * half_len, kv_all.shape[2]
                )

            def score(keys):
                return lax.dot_general(
                    queries_ref[...],
                    keys,
                    (((1,), (1,)), ((), ())),
                    preferred_element_type=jnp.float32,
                )

            allowed = key_pos_ref[int(upper) : int(upper) + 1] <= query_pos
            parts = [jnp.where(allowed, score(rows_of(int(upper))), masked_score)]
            peak = jnp.max(parts[0], axis=-1, keepdims=True)
            if upper:
                parts.append(score(rows_of(0)))
                peak = jnp.maximum(peak, jnp.max(parts[1], axis=-1, keepdims=True))
            total, weighted = 0.0, 0.0
            for half, part in zip((int(upper), 0), parts):
                weights = jnp.exp2((part - peak) * factor)
                total += jnp.sum(weights, axis=-1, keepdims=True)
                weighted += jnp.dot(
                    weights.astype(jnp.bfloat16),
                    rows_of(half)[:, :latent_width],
                    preferred_element_type=jnp.float32,
                )
            queries_ref[:, :latent_width] = (weighted / total).astype(jnp.bfloat16)

        pl.when(block < halves)(functools.partial(attend, False))
        pl.when(block >= halves)(functools.partial(attend, True))
        for head in range(head_count):
            out_ref[block, :, head * value_width : (head + 1) * value_width] = jnp.dot(
                queries_ref[head * rows : (head + 1) * rows, :latent_width],
                absorb_value_ref[head],
                preferred_element_type=jnp.float32,
            ).astype(jnp.bfloat16)

        @pl.when(step < last)
        def _():
            @pl.when(step + 1 > norm_reach)
            def _():
                norm_step(step + 1)

            project(block_at(step + 1))

        return carry

    lax.fori_loop(0, head_devices, block_body, 0)

    for condition, copy in sent:
        when(condition, copy.wait_send)
    for far in range(1, norm_reach + 1):
        when(z + far <= last, norm_copy(z, 1, far).wait_send)
        when(z >= far, norm_copy(z, -1, far).wait_send)
    for step in range(norm_reach, last):
        when(both(z >= step, z < last), norm_copy(z - step, 1).wait_send)
        when(both(z + step <= last, z > 0), norm_copy(z + step, -1).wait_send)


def per_device(query_latent, norm_gain, kv_latent, q_up, absorb_key, absorb_value, block_owner):
    head_devices = lax.axis_size("head")
    ctx_count = lax.axis_size("ctx")
    rows, query_width = query_latent.shape
    kv_width = kv_latent.shape[1]
    head_count, _, value_width = absorb_value.shape
    padded_width = 128 * pl.cdiv(kv_width, 128)
    rope_half = (kv_width - absorb_key.shape[2]) // 2
    tok_dev = rows * head_devices
    piece_count = ctx_count * head_devices
    bits = (ctx_count // 2).bit_length() - 1
    slots = head_devices * ((ctx_count // 2) * (bits + 1) * 2 + 8)
    bf16, f32 = jnp.bfloat16, jnp.float32
    whole = pl.BlockSpec(memory_space=pltpu.VMEM)
    away = pl.BlockSpec(memory_space=pl.ANY)
    out = pl.pallas_call(
        functools.partial(kernel, ctx_count, head_devices),
        out_shape=jax.ShapeDtypeStruct((head_devices, rows, head_count * value_width), bf16),
        in_specs=[pl.BlockSpec(memory_space=pltpu.SMEM)] + [away] * 6,
        out_specs=whole,
        scratch_shapes=[
            pltpu.VMEM(kv_latent.shape, bf16),
            pltpu.VMEM(query_latent.shape, bf16),
            pltpu.VMEM(norm_gain.shape, bf16),
            pltpu.VMEM(q_up.shape, bf16),
            pltpu.VMEM(absorb_key.shape, bf16),
            pltpu.VMEM(absorb_value.shape, bf16),
            pltpu.VMEM((piece_count, rows, padded_width), bf16),
            pltpu.VMEM((head_devices, rows, query_width), bf16),
            pltpu.VMEM((tok_dev, rope_half), f32),
            pltpu.VMEM((tok_dev, rope_half), f32),
            pltpu.VMEM((2, ctx_count * tok_dev // 2), jnp.int32),
            pltpu.VMEM((rows, q_up.shape[1]), f32),
            pltpu.VMEM((head_count * rows, padded_width), bf16),
            pltpu.SemaphoreType.DMA((piece_count,)),
            pltpu.SemaphoreType.DMA((slots,)),
            pltpu.SemaphoreType.DMA((head_devices,)),
            pltpu.SemaphoreType.DMA((head_devices + 2,)),
            pltpu.SemaphoreType.DMA((head_devices + 2,)),
            pltpu.SemaphoreType.DMA((6,)),
        ],
        compiler_params=pltpu.CompilerParams(
            collective_id=0, has_side_effects=True, vmem_limit_bytes=60 * 1024 * 1024
        ),
    )(
        block_owner,
        query_latent,
        norm_gain,
        kv_latent,
        q_up,
        absorb_key,
        absorb_value,
    )
    return out.reshape(tok_dev, head_count * value_width)


def solution(mesh):
    return jax.shard_map(
        per_device,
        mesh=mesh,
        in_specs=(
            P(("ctx", "head"), None),
            P(),
            P(("ctx", "head"), None),
            P(None, "head"),
            P("head", None, None),
            P("head", None, None),
            P(),
        ),
        out_specs=P("ctx", "head"),
        check_vma=False,
    )
```

```python
import functools
import math

import jax
import jax.numpy as jnp
from jax import lax
from jax.experimental import pallas as pl
from jax.experimental.pallas import tpu as pltpu
from jax.sharding import PartitionSpec as P

epsilon = 1e-06
masked_score = -1e30
MESH = pl.DeviceIdType.MESH


def when(condition, action):
    if condition is True:
        action()
    else:
        pl.when(condition)(action)


def both(first, second):
    if first is True:
        return second
    if second is True:
        return first
    return jnp.logical_and(first, second)


def kernel(
    ctx_count,
    head_devices,
    owner_ref,
    query_hbm,
    gain_hbm,
    kv_hbm,
    q_up_hbm,
    absorb_key_hbm,
    absorb_value_hbm,
    out_ref,
    query_ref,
    gain_ref,
    q_up_ref,
    absorb_key_ref,
    absorb_value_ref,
    kv_all,
    normed_all,
    cosine_ref,
    sine_ref,
    key_pos_ref,
    projected_ref,
    queries_ref,
    kv_recv,
    kv_send,
    norm_recv,
    norm_send_up,
    norm_send_down,
    load_sem,
):
    rows = query_ref.shape[0]
    head_count, nope_width, latent_width = absorb_key_ref.shape
    value_width = absorb_value_ref.shape[2]
    head_width = q_up_ref.shape[1] // head_count
    rope_width = head_width - nope_width
    half_width = rope_width // 2
    tok_dev = rows * head_devices
    half_len = tok_dev // 2
    chips = ctx_count // 2
    bits = chips.bit_length() - 1
    last = head_devices - 1
    ctx = lax.axis_index("ctx")
    z = lax.axis_index("head")

    def across(relative):
        place = ctx
        for bit in range(bits):
            if (relative >> bit) & 1:
                weight = 2 ** (bit + 1)
                place = place + weight - 2 * weight * lax.rem(lax.div(ctx, weight), 2)
        return place

    def other_core(place):
        return place + 1 - 2 * lax.rem(place, 2)

    sibling = other_core(ctx)

    halves = head_devices // 2
    half_pieces = ctx_count * halves

    def slot_of(origin, piece):
        return lax.div(piece, halves) * half_pieces + origin * halves + lax.rem(piece, halves)

    loads = [
        pltpu.make_async_copy(kv_hbm, kv_all.at[slot_of(ctx, z)], load_sem.at[3]),
        pltpu.make_async_copy(query_hbm, query_ref, load_sem.at[4]),
        pltpu.make_async_copy(gain_hbm, gain_ref, load_sem.at[5]),
        pltpu.make_async_copy(q_up_hbm, q_up_ref, load_sem.at[0]),
        pltpu.make_async_copy(absorb_key_hbm, absorb_key_ref, load_sem.at[1]),
        pltpu.make_async_copy(absorb_value_hbm, absorb_value_ref, load_sem.at[2]),
    ]

    for load in loads:
        load.start()

    barrier = pltpu.get_barrier_semaphore()
    for bit in range(bits):
        pl.semaphore_signal(barrier, inc=1, device_id=(across(1 << bit), z), device_id_type=MESH)
    pl.semaphore_signal(barrier, inc=1, device_id=(sibling, z), device_id_type=MESH)

    kv_reach = min(2, last)
    norm_reach = min(1, last)
    partners = bits + 1
    for step in range(1, kv_reach + 1):
        for valid, place in ((z + step <= last, z + step), (z >= step, z - step)):
            partners = partners + jnp.where(valid, 1, 0)
            when(
                valid,
                functools.partial(
                    pl.semaphore_signal,
                    barrier,
                    inc=1,
                    device_id=(ctx, place),
                    device_id_type=MESH,
                ),
            )

    loads[0].wait()
    pl.semaphore_wait(barrier, partners)

    sent = []

    def kv_copy(origin, piece, slot, target):
        index = slot_of(origin, piece)
        return pltpu.make_async_remote_copy(
            src_ref=kv_all.at[index],
            dst_ref=kv_all.at[index],
            send_sem=kv_send.at[slot],
            recv_sem=kv_recv.at[index],
            device_id=target,
            device_id_type=MESH,
        )

    def send_kv(condition, origin, piece, target):
        copy = kv_copy(origin, piece, len(sent), target)
        sent.append((condition, copy))
        when(condition, copy.start)

    def wait_kv(condition, origin, piece):
        when(condition, kv_copy(origin, piece, 0, (sibling, z)).wait_recv)

    def pieces(step):
        if step == 0:
            return [(True, z, 0)]
        return [(z >= step, z - step, 1), (z + step <= last, z + step, -1)]

    def own_block(step):
        if step == 0:
            for far in range(1, kv_reach + 1):
                send_kv(z + far <= last, ctx, z, (ctx, z + far))
                send_kv(z >= far, ctx, z, (ctx, z - far))
        for valid, piece, way in pieces(step):
            if step > 0:
                wait_kv(valid, ctx, piece)
            if kv_reach <= step < last:
                onward = z < last if way > 0 else z > 0
                send_kv(both(valid, onward), ctx, piece, (ctx, z + way))
            for bit in range(bits):
                send_kv(valid, ctx, piece, (across(1 << bit), z))
            send_kv(valid, ctx, piece, (sibling, z))

    def relay(step, relative):
        origin = across(relative)
        for valid, piece, _ in pieces(step):
            wait_kv(valid, origin, piece)
            even = lax.rem(piece + head_devices, 2) == 0
            for bit in range(bits):
                if relative < (1 << bit):
                    send_kv(both(valid, even), origin, piece, (across(1 << bit), z))
                elif relative & ((2 << bit) - 1) == 0:
                    odd = jnp.logical_not(even)
                    send_kv(both(valid, odd), origin, piece, (across(1 << bit), z))
            send_kv(valid, origin, piece, (sibling, z))

    def norm_copy(block, way, far=1):
        send_sem = norm_send_up if way > 0 else norm_send_down
        return pltpu.make_async_remote_copy(
            src_ref=normed_all.at[block],
            dst_ref=normed_all.at[block],
            send_sem=send_sem.at[block if far == 1 else last + far],
            recv_sem=norm_recv.at[block],
            device_id=(ctx, z + far * way),
            device_id_type=MESH,
        )

    def norm_step(step):
        for valid, block, way, onward in (
            (z >= step, z - step, 1, z < last),
            (z + step <= last, z + step, -1, z > 0),
        ):
            copy = norm_copy(block, way)
            when(valid, copy.wait_recv)
            when(both(valid, jnp.logical_and(onward, step >= norm_reach)), copy.start)

    own_block(0)
    loads[1].wait()
    loads[2].wait()
    query_f32 = query_ref[...].astype(jnp.float32)
    normed_all[z] = (
        query_f32
        * lax.rsqrt(jnp.mean(query_f32 * query_f32, axis=-1, keepdims=True) + epsilon)
        * gain_ref[...].reshape(1, -1).astype(jnp.float32)
    ).astype(jnp.bfloat16)

    for far in range(1, norm_reach + 1):
        when(z + far <= last, norm_copy(z, 1, far).start)
        when(z >= far, norm_copy(z, -1, far).start)

    def half_base(owner, upper):
        return jnp.where(upper, 2 * ctx_count - 1 - owner, owner) * half_len

    def tables():
        own = owner_ref[ctx]
        groups = 128 // half_width
        span = tok_dev // groups
        lanes = lax.broadcasted_iota(jnp.int32, (span, 128), 1)
        offset = lax.broadcasted_iota(jnp.int32, (span, 128), 0) + span * lax.div(
            lanes, half_width
        )
        places = jnp.where(
            offset < half_len,
            own * half_len + offset,
            (2 * ctx_count - 1 - own) * half_len + offset - half_len,
        )
        frequency = jnp.exp(
            lax.rem(lanes[:1], half_width).astype(jnp.float32)
            * (-math.log(10000.0) / half_width)
        )
        angles = places.astype(jnp.float32) * frequency
        cosine, sine = jnp.cos(angles), jnp.sin(angles)
        for group in range(groups):
            begin = group * half_width
            cosine_ref[group * span : (group + 1) * span] = cosine[:, begin : begin + half_width]
            sine_ref[group * span : (group + 1) * span] = sine[:, begin : begin + half_width]
        lane = lax.broadcasted_iota(jnp.int32, (1, half_len), 1)
        for index in range(ctx_count):
            owner = owner_ref[index]
            columns = slice(index * half_len, (index + 1) * half_len)
            key_pos_ref[:1, columns] = owner * half_len + lane
            key_pos_ref[1:, columns] = (2 * ctx_count - 1 - owner) * half_len + lane

    distances = [
        [r for r in range(chips) if bin(r).count("1") == level] for level in range(bits + 1)
    ]
    for stage in range(head_devices + bits):
        if 0 < stage < head_devices:
            own_block(stage)
        for level in range(1, bits + 1):
            if 0 <= stage - level < head_devices:
                for relative in distances[level]:
                    relay(stage - level, relative)
        if stage == 0:
            tables()
    for step in range(1, norm_reach + 1):
        norm_step(step)
    for load in loads[3:]:
        load.wait()

    factor = float(head_width) ** (-0.5) * math.log2(math.e)
    shorter = jnp.minimum(z, last - z)

    def block_at(step):
        near = z + lax.div(step + 1, 2) * (1 - 2 * lax.rem(step, 2))
        far = jnp.where(z > last - z, last - step, step)
        return jnp.where(step <= 2 * shorter, near, far)

    def project(block):
        projected_ref[...] = jnp.dot(
            normed_all[block], q_up_ref[...], preferred_element_type=jnp.float32
        )
        cosine = cosine_ref[pl.ds(pl.multiple_of(block * rows, rows), rows)]
        sine = sine_ref[pl.ds(pl.multiple_of(block * rows, rows), rows)]
        for head in range(head_count):
            begin = head * head_width
            q_nope = projected_ref[:, begin : begin + nope_width].astype(jnp.bfloat16)
            q_abs = jnp.dot(q_nope, absorb_key_ref[head], preferred_element_type=jnp.float32)
            begin += nope_width
            front = projected_ref[:, begin : begin + half_width]
            back = projected_ref[:, begin + half_width : begin + rope_width]
            span = slice(head * rows, (head + 1) * rows)
            queries_ref[span, :latent_width] = q_abs.astype(jnp.bfloat16)
            queries_ref[span, latent_width:] = jnp.concatenate(
                [front * cosine - back * sine, front * sine + back * cosine], axis=-1
            ).astype(jnp.bfloat16)

    project(z)
    for relative in range(chips):
        for piece in range(head_devices):
            wait_kv(True, other_core(across(relative)), piece)

    def block_body(step, carry):
        block = block_at(step)
        offset = block * rows
        base = half_base(owner_ref[ctx], offset >= half_len) + lax.rem(offset, half_len)
        query_pos = base + lax.rem(
            lax.broadcasted_iota(jnp.int32, (head_count * rows, 1), 0), rows
        )

        def attend(upper):
            def rows_of(half):
                return kv_all[half * half_pieces : (half + 1) * half_pieces].reshape(
                    ctx_count * half_len, latent_width + rope_width
                )

            def score(keys):
                return lax.dot_general(
                    queries_ref[...],
                    keys,
                    (((1,), (1,)), ((), ())),
                    preferred_element_type=jnp.float32,
                )

            allowed = key_pos_ref[int(upper) : int(upper) + 1] <= query_pos
            parts = [jnp.where(allowed, score(rows_of(int(upper))), masked_score)]
            peak = jnp.max(parts[0], axis=-1, keepdims=True)
            if upper:
                parts.append(score(rows_of(0)))
                peak = jnp.maximum(peak, jnp.max(parts[1], axis=-1, keepdims=True))
            total, weighted = 0.0, 0.0
            for half, part in zip((int(upper), 0), parts):
                weights = jnp.exp2((part - peak) * factor)
                total += jnp.sum(weights, axis=-1, keepdims=True)
                weighted += jnp.dot(
                    weights.astype(jnp.bfloat16),
                    rows_of(half)[:, :latent_width],
                    preferred_element_type=jnp.float32,
                )
            queries_ref[:, :latent_width] = (weighted / total).astype(jnp.bfloat16)

        pl.when(block < halves)(functools.partial(attend, False))
        pl.when(block >= halves)(functools.partial(attend, True))
        for head in range(head_count):
            out_ref[block, :, head * value_width : (head + 1) * value_width] = jnp.dot(
                queries_ref[head * rows : (head + 1) * rows, :latent_width],
                absorb_value_ref[head],
                preferred_element_type=jnp.float32,
            ).astype(jnp.bfloat16)

        @pl.when(step + 2 < last)
        def _():
            norm_step(step + 2)

        @pl.when(step < last)
        def _():
            if last > 1:
                @pl.when(step + 1 == last)
                def _():
                    norm_step(last)

            project(block_at(step + 1))

        return carry

    lax.fori_loop(0, head_devices, block_body, 0)

    for condition, copy in sent:
        when(condition, copy.wait_send)
    for far in range(1, norm_reach + 1):
        when(z + far <= last, norm_copy(z, 1, far).wait_send)
        when(z >= far, norm_copy(z, -1, far).wait_send)
    for step in range(norm_reach, last):
        when(both(z >= step, z < last), norm_copy(z - step, 1).wait_send)
        when(both(z + step <= last, z > 0), norm_copy(z + step, -1).wait_send)


def per_device(query_latent, norm_gain, kv_latent, q_up, absorb_key, absorb_value, block_owner):
    head_devices = lax.axis_size("head")
    ctx_count = lax.axis_size("ctx")
    rows, query_width = query_latent.shape
    kv_width = kv_latent.shape[1]
    head_count, _, value_width = absorb_value.shape
    rope_half = (kv_width - absorb_key.shape[2]) // 2
    tok_dev = rows * head_devices
    piece_count = ctx_count * head_devices
    bits = (ctx_count // 2).bit_length() - 1
    slots = head_devices * ((ctx_count // 2) * (bits + 1) * 2 + 8)
    bf16, f32 = jnp.bfloat16, jnp.float32
    whole = pl.BlockSpec(memory_space=pltpu.VMEM)
    away = pl.BlockSpec(memory_space=pl.ANY)
    out = pl.pallas_call(
        functools.partial(kernel, ctx_count, head_devices),
        out_shape=jax.ShapeDtypeStruct((head_devices, rows, head_count * value_width), bf16),
        in_specs=[pl.BlockSpec(memory_space=pltpu.SMEM)] + [away] * 6,
        out_specs=whole,
        scratch_shapes=[
            pltpu.VMEM(query_latent.shape, bf16),
            pltpu.VMEM(norm_gain.shape, bf16),
            pltpu.VMEM(q_up.shape, bf16),
            pltpu.VMEM(absorb_key.shape, bf16),
            pltpu.VMEM(absorb_value.shape, bf16),
            pltpu.VMEM((piece_count, rows, kv_width), bf16),
            pltpu.VMEM((head_devices, rows, query_width), bf16),
            pltpu.VMEM((tok_dev, rope_half), f32),
            pltpu.VMEM((tok_dev, rope_half), f32),
            pltpu.VMEM((2, ctx_count * tok_dev // 2), jnp.int32),
            pltpu.VMEM((rows, q_up.shape[1]), f32),
            pltpu.VMEM((head_count * rows, kv_width), bf16),
            pltpu.SemaphoreType.DMA((piece_count,)),
            pltpu.SemaphoreType.DMA((slots,)),
            pltpu.SemaphoreType.DMA((head_devices,)),
            pltpu.SemaphoreType.DMA((head_devices + 2,)),
            pltpu.SemaphoreType.DMA((head_devices + 2,)),
            pltpu.SemaphoreType.DMA((6,)),
        ],
        compiler_params=pltpu.CompilerParams(
            collective_id=0, has_side_effects=True, vmem_limit_bytes=60 * 1024 * 1024
        ),
    )(
        block_owner,
        query_latent,
        norm_gain,
        kv_latent,
        q_up,
        absorb_key,
        absorb_value,
    )
    return out.reshape(tok_dev, head_count * value_width)


def solution(mesh):
    return jax.shard_map(
        per_device,
        mesh=mesh,
        in_specs=(
            P(("ctx", "head"), None),
            P(),
            P(("ctx", "head"), None),
            P(None, "head"),
            P("head", None, None),
            P("head", None, None),
            P(),
        ),
        out_specs=P("ctx", "head"),
        check_vma=False,
    )
```

```python
import functools
import math

import jax
import jax.numpy as jnp
from jax import lax
from jax.experimental import pallas as pl
from jax.experimental.pallas import tpu as pltpu
from jax.sharding import PartitionSpec as P

epsilon = 1e-06
masked_score = -1e30
MESH = pl.DeviceIdType.MESH


def when(condition, action):
    if condition is True:
        action()
    else:
        pl.when(condition)(action)


def both(first, second):
    if first is True:
        return second
    if second is True:
        return first
    return jnp.logical_and(first, second)


def kernel(
    ctx_count,
    head_devices,
    owner_ref,
    query_hbm,
    gain_hbm,
    kv_hbm,
    q_up_hbm,
    absorb_key_hbm,
    absorb_value_hbm,
    out_ref,
    query_ref,
    gain_ref,
    q_up_ref,
    absorb_key_ref,
    absorb_value_ref,
    kv_all,
    normed_all,
    cosine_ref,
    sine_ref,
    key_pos_ref,
    projected_ref,
    queries_ref,
    kv_recv,
    kv_send,
    norm_recv,
    norm_send_up,
    norm_send_down,
    load_sem,
):
    rows = query_ref.shape[0]
    head_count, nope_width, latent_width = absorb_key_ref.shape
    value_width = absorb_value_ref.shape[2]
    head_width = q_up_ref.shape[1] // head_count
    rope_width = head_width - nope_width
    half_width = rope_width // 2
    tok_dev = rows * head_devices
    half_len = tok_dev // 2
    chips = ctx_count // 2
    bits = chips.bit_length() - 1
    last = head_devices - 1
    ctx = lax.axis_index("ctx")
    z = lax.axis_index("head")

    def across(relative):
        place = ctx
        for bit in range(bits):
            if (relative >> bit) & 1:
                weight = 2 ** (bit + 1)
                place = place + weight - 2 * weight * lax.rem(lax.div(ctx, weight), 2)
        return place

    def other_core(place):
        return place + 1 - 2 * lax.rem(place, 2)

    sibling = other_core(ctx)

    halves = head_devices // 2
    half_pieces = ctx_count * halves

    def slot_of(origin, piece):
        return lax.div(piece, halves) * half_pieces + origin * halves + lax.rem(piece, halves)

    loads = [
        pltpu.make_async_copy(kv_hbm, kv_all.at[slot_of(ctx, z)], load_sem.at[3]),
        pltpu.make_async_copy(query_hbm, query_ref, load_sem.at[4]),
        pltpu.make_async_copy(gain_hbm, gain_ref, load_sem.at[5]),
        pltpu.make_async_copy(q_up_hbm, q_up_ref, load_sem.at[0]),
        pltpu.make_async_copy(absorb_key_hbm, absorb_key_ref, load_sem.at[1]),
        pltpu.make_async_copy(absorb_value_hbm, absorb_value_ref, load_sem.at[2]),
    ]

    for load in loads:
        load.start()

    barrier = pltpu.get_barrier_semaphore()
    for bit in range(bits):
        pl.semaphore_signal(barrier, inc=1, device_id=(across(1 << bit), z), device_id_type=MESH)
    pl.semaphore_signal(barrier, inc=1, device_id=(sibling, z), device_id_type=MESH)

    kv_reach = min(2, last)
    norm_reach = min(1, last)
    partners = bits + 1
    for step in range(1, kv_reach + 1):
        for valid, place in ((z + step <= last, z + step), (z >= step, z - step)):
            partners = partners + jnp.where(valid, 1, 0)
            when(
                valid,
                functools.partial(
                    pl.semaphore_signal,
                    barrier,
                    inc=1,
                    device_id=(ctx, place),
                    device_id_type=MESH,
                ),
            )

    loads[0].wait()
    pl.semaphore_wait(barrier, partners)

    sent = []

    def kv_copy(origin, piece, slot, target):
        index = slot_of(origin, piece)
        return pltpu.make_async_remote_copy(
            src_ref=kv_all.at[index],
            dst_ref=kv_all.at[index],
            send_sem=kv_send.at[slot],
            recv_sem=kv_recv.at[index],
            device_id=target,
            device_id_type=MESH,
        )

    def send_kv(condition, origin, piece, target):
        copy = kv_copy(origin, piece, len(sent), target)
        sent.append((condition, copy))
        when(condition, copy.start)

    def wait_kv(condition, origin, piece):
        when(condition, kv_copy(origin, piece, 0, (sibling, z)).wait_recv)

    def pieces(step):
        if step == 0:
            return [(True, z, 0)]
        return [(z >= step, z - step, 1), (z + step <= last, z + step, -1)]

    def own_block(step):
        if step == 0:
            for far in range(1, kv_reach + 1):
                send_kv(z + far <= last, ctx, z, (ctx, z + far))
                send_kv(z >= far, ctx, z, (ctx, z - far))
        for valid, piece, way in pieces(step):
            if step > 0:
                wait_kv(valid, ctx, piece)
            if kv_reach <= step < last:
                onward = z < last if way > 0 else z > 0
                send_kv(both(valid, onward), ctx, piece, (ctx, z + way))
            for bit in range(bits):
                send_kv(valid, ctx, piece, (across(1 << bit), z))
            send_kv(valid, ctx, piece, (sibling, z))

    def relay(step, relative):
        origin = across(relative)
        for valid, piece, _ in pieces(step):
            wait_kv(valid, origin, piece)
            even = lax.rem(piece + head_devices, 2) == 0
            for bit in range(bits):
                if relative < (1 << bit):
                    send_kv(both(valid, even), origin, piece, (across(1 << bit), z))
                elif relative & ((2 << bit) - 1) == 0:
                    odd = jnp.logical_not(even)
                    send_kv(both(valid, odd), origin, piece, (across(1 << bit), z))
            send_kv(valid, origin, piece, (sibling, z))

    def normed_at(block):
        begin = pl.multiple_of(lax.rem(block, 2) * rows, rows)
        return normed_all.at[lax.div(block, 2), pl.ds(begin, rows)]

    def norm_copy(block, way, far=1):
        send_sem = norm_send_up if way > 0 else norm_send_down
        return pltpu.make_async_remote_copy(
            src_ref=normed_at(block),
            dst_ref=normed_at(block),
            send_sem=send_sem.at[block if far == 1 else last + far],
            recv_sem=norm_recv.at[block],
            device_id=(ctx, z + far * way),
            device_id_type=MESH,
        )

    def norm_step(step):
        for valid, block, way, onward in (
            (z >= step, z - step, 1, z < last),
            (z + step <= last, z + step, -1, z > 0),
        ):
            copy = norm_copy(block, way)
            when(valid, copy.wait_recv)
            when(both(valid, jnp.logical_and(onward, step >= norm_reach)), copy.start)

    own_block(0)
    loads[1].wait()
    loads[2].wait()
    query_f32 = query_ref[...].astype(jnp.float32)
    normed_at(z)[...] = (
        query_f32
        * lax.rsqrt(jnp.mean(query_f32 * query_f32, axis=-1, keepdims=True) + epsilon)
        * gain_ref[...].reshape(1, -1).astype(jnp.float32)
    ).astype(jnp.bfloat16)

    for far in range(1, norm_reach + 1):
        when(z + far <= last, norm_copy(z, 1, far).start)
        when(z >= far, norm_copy(z, -1, far).start)

    def half_base(owner, upper):
        return jnp.where(upper, 2 * ctx_count - 1 - owner, owner) * half_len

    def tables():
        own = owner_ref[ctx]
        groups = 128 // half_width
        span = tok_dev // groups
        lanes = lax.broadcasted_iota(jnp.int32, (span, 128), 1)
        offset = lax.broadcasted_iota(jnp.int32, (span, 128), 0) + span * lax.div(
            lanes, half_width
        )
        places = jnp.where(
            offset < half_len,
            own * half_len + offset,
            (2 * ctx_count - 1 - own) * half_len + offset - half_len,
        )
        frequency = jnp.exp(
            lax.rem(lanes[:1], half_width).astype(jnp.float32)
            * (-math.log(10000.0) / half_width)
        )
        angles = places.astype(jnp.float32) * frequency
        cosine, sine = jnp.cos(angles), jnp.sin(angles)
        for group in range(groups):
            begin = group * half_width
            cosine_ref[group * span : (group + 1) * span] = cosine[:, begin : begin + half_width]
            sine_ref[group * span : (group + 1) * span] = sine[:, begin : begin + half_width]
        lane = lax.broadcasted_iota(jnp.int32, (1, half_len), 1)
        for index in range(ctx_count):
            owner = owner_ref[index]
            columns = slice(index * half_len, (index + 1) * half_len)
            key_pos_ref[:1, columns] = owner * half_len + lane
            key_pos_ref[1:, columns] = (2 * ctx_count - 1 - owner) * half_len + lane

    distances = [
        [r for r in range(chips) if bin(r).count("1") == level] for level in range(bits + 1)
    ]
    for stage in range(head_devices + bits):
        if 0 < stage < head_devices:
            own_block(stage)
        for level in range(1, bits + 1):
            if 0 <= stage - level < head_devices:
                for relative in distances[level]:
                    relay(stage - level, relative)
        if stage == 0:
            tables()
    norm_step(1)
    for load in loads[3:]:
        load.wait()

    factor = float(head_width) ** (-0.5) * math.log2(math.e)
    pair_rows = 2 * rows
    own_pair = lax.div(z, 2)
    last_pair = last // 2
    shorter = jnp.minimum(own_pair, last_pair - own_pair)

    def pair_at(step):
        near = own_pair + lax.div(step + 1, 2) * (1 - 2 * lax.rem(step, 2))
        far = jnp.where(own_pair > last_pair - own_pair, last_pair - step, step)
        return jnp.where(step <= 2 * shorter, near, far)

    def project(pair):
        projected_ref[...] = jnp.dot(
            normed_all[pair], q_up_ref[...], preferred_element_type=jnp.float32
        )
        cosine = cosine_ref[pl.ds(pl.multiple_of(pair * pair_rows, pair_rows), pair_rows)]
        sine = sine_ref[pl.ds(pl.multiple_of(pair * pair_rows, pair_rows), pair_rows)]
        for head in range(head_count):
            begin = head * head_width
            q_nope = projected_ref[:, begin : begin + nope_width].astype(jnp.bfloat16)
            q_abs = jnp.dot(q_nope, absorb_key_ref[head], preferred_element_type=jnp.float32)
            begin += nope_width
            front = projected_ref[:, begin : begin + half_width]
            back = projected_ref[:, begin + half_width : begin + rope_width]
            span = slice(head * pair_rows, (head + 1) * pair_rows)
            queries_ref[span, :latent_width] = q_abs.astype(jnp.bfloat16)
            queries_ref[span, latent_width:] = jnp.concatenate(
                [front * cosine - back * sine, front * sine + back * cosine], axis=-1
            ).astype(jnp.bfloat16)

    project(own_pair)
    for relative in range(chips):
        for piece in range(head_devices):
            wait_kv(True, other_core(across(relative)), piece)

    if last > 1:
        norm_step(2)

    def pair_body(step, carry):
        pair = pair_at(step)
        offset = pair * pair_rows
        base = half_base(owner_ref[ctx], offset >= half_len) + lax.rem(offset, half_len)
        query_pos = base + lax.rem(
            lax.broadcasted_iota(jnp.int32, (head_count * pair_rows, 1), 0), pair_rows
        )

        def attend(upper):
            def rows_of(half):
                return kv_all[half * half_pieces : (half + 1) * half_pieces].reshape(
                    ctx_count * half_len, latent_width + rope_width
                )

            def score(keys):
                return lax.dot_general(
                    queries_ref[...],
                    keys,
                    (((1,), (1,)), ((), ())),
                    preferred_element_type=jnp.float32,
                )

            allowed = key_pos_ref[int(upper) : int(upper) + 1] <= query_pos
            parts = [jnp.where(allowed, score(rows_of(int(upper))), masked_score)]
            peak = jnp.max(parts[0], axis=-1, keepdims=True)
            if upper:
                parts.append(score(rows_of(0)))
                peak = jnp.maximum(peak, jnp.max(parts[1], axis=-1, keepdims=True))
            total, weighted = 0.0, 0.0
            for half, part in zip((int(upper), 0), parts):
                weights = jnp.exp2((part - peak) * factor)
                total += jnp.sum(weights, axis=-1, keepdims=True)
                weighted += jnp.dot(
                    weights.astype(jnp.bfloat16),
                    rows_of(half)[:, :latent_width],
                    preferred_element_type=jnp.float32,
                )
            queries_ref[:, :latent_width] = (weighted / total).astype(jnp.bfloat16)

        pl.when(2 * pair < halves)(functools.partial(attend, False))
        pl.when(2 * pair >= halves)(functools.partial(attend, True))
        for head in range(head_count):
            out_ref[pair, :, head * value_width : (head + 1) * value_width] = jnp.dot(
                queries_ref[head * pair_rows : (head + 1) * pair_rows, :latent_width],
                absorb_value_ref[head],
                preferred_element_type=jnp.float32,
            ).astype(jnp.bfloat16)

        @pl.when(step < last_pair)
        def _():
            norm_step(2 * step + 3)

            @pl.when(2 * step + 4 <= last)
            def _():
                norm_step(2 * step + 4)

            project(pair_at(step + 1))

        return carry

    lax.fori_loop(0, head_devices // 2, pair_body, 0)

    for condition, copy in sent:
        when(condition, copy.wait_send)
    for far in range(1, norm_reach + 1):
        when(z + far <= last, norm_copy(z, 1, far).wait_send)
        when(z >= far, norm_copy(z, -1, far).wait_send)
    for step in range(norm_reach, last):
        when(both(z >= step, z < last), norm_copy(z - step, 1).wait_send)
        when(both(z + step <= last, z > 0), norm_copy(z + step, -1).wait_send)


def per_device(query_latent, norm_gain, kv_latent, q_up, absorb_key, absorb_value, block_owner):
    head_devices = lax.axis_size("head")
    ctx_count = lax.axis_size("ctx")
    rows, query_width = query_latent.shape
    kv_width = kv_latent.shape[1]
    head_count, _, value_width = absorb_value.shape
    rope_half = (kv_width - absorb_key.shape[2]) // 2
    tok_dev = rows * head_devices
    piece_count = ctx_count * head_devices
    bits = (ctx_count // 2).bit_length() - 1
    slots = head_devices * ((ctx_count // 2) * (bits + 1) * 2 + 8)
    bf16, f32 = jnp.bfloat16, jnp.float32
    whole = pl.BlockSpec(memory_space=pltpu.VMEM)
    away = pl.BlockSpec(memory_space=pl.ANY)
    out = pl.pallas_call(
        functools.partial(kernel, ctx_count, head_devices),
        out_shape=jax.ShapeDtypeStruct((head_devices // 2, 2 * rows, head_count * value_width), bf16),
        in_specs=[pl.BlockSpec(memory_space=pltpu.SMEM)] + [away] * 6,
        out_specs=whole,
        scratch_shapes=[
            pltpu.VMEM(query_latent.shape, bf16),
            pltpu.VMEM(norm_gain.shape, bf16),
            pltpu.VMEM(q_up.shape, bf16),
            pltpu.VMEM(absorb_key.shape, bf16),
            pltpu.VMEM(absorb_value.shape, bf16),
            pltpu.VMEM((piece_count, rows, kv_width), bf16),
            pltpu.VMEM((head_devices // 2, 2 * rows, query_width), bf16),
            pltpu.VMEM((tok_dev, rope_half), f32),
            pltpu.VMEM((tok_dev, rope_half), f32),
            pltpu.VMEM((2, ctx_count * tok_dev // 2), jnp.int32),
            pltpu.VMEM((2 * rows, q_up.shape[1]), f32),
            pltpu.VMEM((2 * head_count * rows, kv_width), bf16),
            pltpu.SemaphoreType.DMA((piece_count,)),
            pltpu.SemaphoreType.DMA((slots,)),
            pltpu.SemaphoreType.DMA((head_devices,)),
            pltpu.SemaphoreType.DMA((head_devices + 2,)),
            pltpu.SemaphoreType.DMA((head_devices + 2,)),
            pltpu.SemaphoreType.DMA((6,)),
        ],
        compiler_params=pltpu.CompilerParams(
            collective_id=0, has_side_effects=True, vmem_limit_bytes=60 * 1024 * 1024
        ),
    )(
        block_owner,
        query_latent,
        norm_gain,
        kv_latent,
        q_up,
        absorb_key,
        absorb_value,
    )
    return out.reshape(tok_dev, head_count * value_width)


def solution(mesh):
    return jax.shard_map(
        per_device,
        mesh=mesh,
        in_specs=(
            P(("ctx", "head"), None),
            P(),
            P(("ctx", "head"), None),
            P(None, "head"),
            P("head", None, None),
            P("head", None, None),
            P(),
        ),
        out_specs=P("ctx", "head"),
        check_vma=False,
    )
```

```python
import functools
import math

import jax
import jax.numpy as jnp
from jax import lax
from jax.experimental import pallas as pl
from jax.experimental.pallas import tpu as pltpu
from jax.sharding import PartitionSpec as P

epsilon = 1e-06
masked_score = -1e30
MESH = pl.DeviceIdType.MESH


def when(condition, action):
    if condition is True:
        action()
    else:
        pl.when(condition)(action)


def both(first, second):
    if first is True:
        return second
    if second is True:
        return first
    return jnp.logical_and(first, second)


def kernel(
    ctx_count,
    head_devices,
    owner_ref,
    query_hbm,
    gain_hbm,
    kv_hbm,
    q_up_hbm,
    absorb_key_hbm,
    absorb_value_hbm,
    out_ref,
    query_ref,
    gain_ref,
    q_up_ref,
    absorb_key_ref,
    absorb_value_ref,
    kv_all,
    normed_all,
    cosine_ref,
    sine_ref,
    key_pos_ref,
    projected_ref,
    queries_ref,
    kv_recv,
    kv_send,
    norm_recv,
    norm_send_up,
    norm_send_down,
    load_sem,
):
    rows = query_ref.shape[0]
    head_count, nope_width, latent_width = absorb_key_ref.shape
    value_width = absorb_value_ref.shape[2]
    head_width = q_up_ref.shape[1] // head_count
    rope_width = head_width - nope_width
    half_width = rope_width // 2
    tok_dev = rows * head_devices
    half_len = tok_dev // 2
    chips = ctx_count // 2
    bits = chips.bit_length() - 1
    last = head_devices - 1
    ctx = lax.axis_index("ctx")
    z = lax.axis_index("head")

    def across(relative):
        place = ctx
        for bit in range(bits):
            if (relative >> bit) & 1:
                weight = 2 ** (bit + 1)
                place = place + weight - 2 * weight * lax.rem(lax.div(ctx, weight), 2)
        return place

    def other_core(place):
        return place + 1 - 2 * lax.rem(place, 2)

    sibling = other_core(ctx)

    halves = head_devices // 2
    half_pieces = ctx_count * halves

    def slot_of(origin, piece):
        return lax.div(piece, halves) * half_pieces + origin * halves + lax.rem(piece, halves)

    loads = [
        pltpu.make_async_copy(kv_hbm, kv_all.at[slot_of(ctx, z)], load_sem.at[3]),
        pltpu.make_async_copy(query_hbm, query_ref, load_sem.at[4]),
        pltpu.make_async_copy(gain_hbm, gain_ref, load_sem.at[5]),
        pltpu.make_async_copy(q_up_hbm, q_up_ref, load_sem.at[0]),
        pltpu.make_async_copy(absorb_key_hbm, absorb_key_ref, load_sem.at[1]),
        pltpu.make_async_copy(absorb_value_hbm, absorb_value_ref, load_sem.at[2]),
    ]

    for load in loads:
        load.start()

    barrier = pltpu.get_barrier_semaphore()
    for bit in range(bits):
        pl.semaphore_signal(barrier, inc=1, device_id=(across(1 << bit), z), device_id_type=MESH)
    pl.semaphore_signal(barrier, inc=1, device_id=(sibling, z), device_id_type=MESH)

    kv_reach = min(2, last)
    partners = bits + 1
    for step in range(1, kv_reach + 1):
        for valid, place in ((z + step <= last, z + step), (z >= step, z - step)):
            partners = partners + jnp.where(valid, 1, 0)
            when(
                valid,
                functools.partial(
                    pl.semaphore_signal,
                    barrier,
                    inc=1,
                    device_id=(ctx, place),
                    device_id_type=MESH,
                ),
            )

    loads[0].wait()
    pl.semaphore_wait(barrier, partners)

    sent = []

    def kv_copy(origin, piece, slot, target):
        index = slot_of(origin, piece)
        return pltpu.make_async_remote_copy(
            src_ref=kv_all.at[index],
            dst_ref=kv_all.at[index],
            send_sem=kv_send.at[slot],
            recv_sem=kv_recv.at[index],
            device_id=target,
            device_id_type=MESH,
        )

    def send_kv(condition, origin, piece, target):
        copy = kv_copy(origin, piece, len(sent), target)
        sent.append((condition, copy))
        when(condition, copy.start)

    def wait_kv(condition, origin, piece):
        when(condition, kv_copy(origin, piece, 0, (sibling, z)).wait_recv)

    def pieces(step):
        if step == 0:
            return [(True, z, 0)]
        return [(z >= step, z - step, 1), (z + step <= last, z + step, -1)]

    def own_block(step):
        if step == 0:
            for far in range(1, kv_reach + 1):
                send_kv(z + far <= last, ctx, z, (ctx, z + far))
                send_kv(z >= far, ctx, z, (ctx, z - far))
        for valid, piece, way in pieces(step):
            if step > 0:
                wait_kv(valid, ctx, piece)
            if kv_reach <= step < last:
                onward = z < last if way > 0 else z > 0
                send_kv(both(valid, onward), ctx, piece, (ctx, z + way))
            for bit in range(bits):
                send_kv(valid, ctx, piece, (across(1 << bit), z))
            send_kv(valid, ctx, piece, (sibling, z))

    def relay(step, relative):
        origin = across(relative)
        for valid, piece, _ in pieces(step):
            wait_kv(valid, origin, piece)
            even = lax.rem(piece + head_devices, 2) == 0
            for bit in range(bits):
                if relative < (1 << bit):
                    send_kv(both(valid, even), origin, piece, (across(1 << bit), z))
                elif relative & ((2 << bit) - 1) == 0:
                    odd = jnp.logical_not(even)
                    send_kv(both(valid, odd), origin, piece, (across(1 << bit), z))
            send_kv(valid, origin, piece, (sibling, z))

    chunks = 2 if rows % 32 == 0 else 1
    chunk_rows = rows // chunks

    def norm_copy(block, way, chunk):
        send_sem = norm_send_up if way > 0 else norm_send_down
        begin = pl.multiple_of(lax.rem(block, 2) * rows + chunk * chunk_rows, chunk_rows)
        view = normed_all.at[lax.div(block, 2), pl.ds(begin, chunk_rows)]
        index = block * chunks + chunk
        return pltpu.make_async_remote_copy(
            src_ref=view,
            dst_ref=view,
            send_sem=send_sem.at[index],
            recv_sem=norm_recv.at[index],
            device_id=(ctx, z + way),
            device_id_type=MESH,
        )

    def norm_blocks(step):
        return (
            (z >= step, z - step, 1, z < last),
            (z + step <= last, z + step, -1, z > 0),
        )

    def norm_forward(step):
        for chunk in range(chunks):
            for valid, block, way, onward in norm_blocks(step):
                copy = norm_copy(block, way, chunk)
                when(both(valid, onward), copy.wait_recv)
                when(both(valid, onward), copy.start)

    def norm_take(step):
        for chunk in range(chunks):
            for valid, block, way, onward in norm_blocks(step):
                here = jnp.logical_and(valid, jnp.logical_not(onward))
                when(here, norm_copy(block, way, chunk).wait_recv)

    own_block(0)
    loads[1].wait()
    loads[2].wait()
    query_f32 = query_ref[...].astype(jnp.float32)
    own_row = pl.multiple_of(lax.rem(z, 2) * rows, rows)
    normed_all[lax.div(z, 2), pl.ds(own_row, rows)] = (
        query_f32
        * lax.rsqrt(jnp.mean(query_f32 * query_f32, axis=-1, keepdims=True) + epsilon)
        * gain_ref[...].reshape(1, -1).astype(jnp.float32)
    ).astype(jnp.bfloat16)

    def send_norm():
        for chunk in range(chunks):
            when(z < last, norm_copy(z, 1, chunk).start)
            when(z > 0, norm_copy(z, -1, chunk).start)

    def half_base(owner, upper):
        return jnp.where(upper, 2 * ctx_count - 1 - owner, owner) * half_len

    def tables():
        own = owner_ref[ctx]
        groups = 128 // half_width
        span = tok_dev // groups
        lanes = lax.broadcasted_iota(jnp.int32, (span, 128), 1)
        offset = lax.broadcasted_iota(jnp.int32, (span, 128), 0) + span * lax.div(
            lanes, half_width
        )
        places = jnp.where(
            offset < half_len,
            own * half_len + offset,
            (2 * ctx_count - 1 - own) * half_len + offset - half_len,
        )
        frequency = jnp.exp(
            lax.rem(lanes[:1], half_width).astype(jnp.float32)
            * (-math.log(10000.0) / half_width)
        )
        angles = places.astype(jnp.float32) * frequency
        cosine, sine = jnp.cos(angles), jnp.sin(angles)
        for group in range(groups):
            begin = group * half_width
            cosine_ref[group * span : (group + 1) * span] = cosine[:, begin : begin + half_width]
            sine_ref[group * span : (group + 1) * span] = sine[:, begin : begin + half_width]
        lane = lax.broadcasted_iota(jnp.int32, (1, half_len), 1)
        for index in range(ctx_count):
            owner = owner_ref[index]
            columns = slice(index * half_len, (index + 1) * half_len)
            key_pos_ref[:1, columns] = owner * half_len + lane
            key_pos_ref[1:, columns] = (2 * ctx_count - 1 - owner) * half_len + lane

    distances = [
        [r for r in range(chips) if bin(r).count("1") == level] for level in range(bits + 1)
    ]
    for stage in range(head_devices + bits):
        if 0 < stage < head_devices:
            own_block(stage)
        for level in range(1, bits + 1):
            if 0 <= stage - level < head_devices:
                for relative in distances[level]:
                    relay(stage - level, relative)
            if stage == last + level == last + 1:
                norm_forward(1)
        if stage == 0:
            tables()
        if stage == min(kv_reach, last):
            send_norm()
    norm_take(1)
    for load in loads[3:]:
        load.wait()

    factor = float(head_width) ** (-0.5) * math.log2(math.e)
    pair_rows = 2 * rows
    own_pair = lax.div(z, 2)
    last_pair = last // 2
    shorter = jnp.minimum(own_pair, last_pair - own_pair)

    def pair_at(step):
        near = own_pair + lax.div(step + 1, 2) * (1 - 2 * lax.rem(step, 2))
        far = jnp.where(own_pair > last_pair - own_pair, last_pair - step, step)
        return jnp.where(step <= 2 * shorter, near, far)

    def project(pair):
        projected_ref[...] = jnp.dot(
            normed_all[pair], q_up_ref[...], preferred_element_type=jnp.float32
        )
        cosine = cosine_ref[pl.ds(pl.multiple_of(pair * pair_rows, pair_rows), pair_rows)]
        sine = sine_ref[pl.ds(pl.multiple_of(pair * pair_rows, pair_rows), pair_rows)]
        for head in range(head_count):
            begin = head * head_width
            q_nope = projected_ref[:, begin : begin + nope_width].astype(jnp.bfloat16)
            q_abs = jnp.dot(q_nope, absorb_key_ref[head], preferred_element_type=jnp.float32)
            begin += nope_width
            front = projected_ref[:, begin : begin + half_width]
            back = projected_ref[:, begin + half_width : begin + rope_width]
            span = slice(head * pair_rows, (head + 1) * pair_rows)
            queries_ref[span, :latent_width] = q_abs.astype(jnp.bfloat16)
            queries_ref[span, latent_width:] = jnp.concatenate(
                [front * cosine - back * sine, front * sine + back * cosine], axis=-1
            ).astype(jnp.bfloat16)

    project(own_pair)
    for relative in range(chips):
        for piece in range(head_devices):
            wait_kv(True, other_core(across(relative)), piece)

    def pair_body(step, carry):
        pair = pair_at(step)
        offset = pair * pair_rows
        base = half_base(owner_ref[ctx], offset >= half_len) + lax.rem(offset, half_len)
        query_pos = base + lax.rem(
            lax.broadcasted_iota(jnp.int32, (head_count * pair_rows, 1), 0), pair_rows
        )

        def attend(upper):
            def rows_of(half):
                return kv_all[half * half_pieces : (half + 1) * half_pieces].reshape(
                    ctx_count * half_len, latent_width + rope_width
                )

            def score(keys):
                return lax.dot_general(
                    queries_ref[...],
                    keys,
                    (((1,), (1,)), ((), ())),
                    preferred_element_type=jnp.float32,
                )

            allowed = key_pos_ref[int(upper) : int(upper) + 1] <= query_pos
            parts = [jnp.where(allowed, score(rows_of(int(upper))), masked_score)]
            peak = jnp.max(parts[0], axis=-1, keepdims=True)
            if upper:
                parts.append(score(rows_of(0)))
                peak = jnp.maximum(peak, jnp.max(parts[1], axis=-1, keepdims=True))

            @pl.when(jnp.logical_and(step == 0, last > 1))
            def _():
                norm_forward(2)

            total, weighted = 0.0, 0.0
            for half, part in zip((int(upper), 0), parts):
                weights = jnp.exp2((part - peak) * factor)
                total += jnp.sum(weights, axis=-1, keepdims=True)
                weighted += jnp.dot(
                    weights.astype(jnp.bfloat16),
                    rows_of(half)[:, :latent_width],
                    preferred_element_type=jnp.float32,
                )
            queries_ref[:, :latent_width] = (weighted / total).astype(jnp.bfloat16)

        pl.when(2 * pair < halves)(functools.partial(attend, False))
        pl.when(2 * pair >= halves)(functools.partial(attend, True))
        for head in range(head_count):
            out_ref[pair, :, head * value_width : (head + 1) * value_width] = jnp.dot(
                queries_ref[head * pair_rows : (head + 1) * pair_rows, :latent_width],
                absorb_value_ref[head],
                preferred_element_type=jnp.float32,
            ).astype(jnp.bfloat16)

        @pl.when(step < last_pair)
        def _():
            norm_take(2 * step + 2)
            for further in (2 * step + 3, 2 * step + 4):
                norm_forward(further)
            norm_take(2 * step + 3)

            project(pair_at(step + 1))

        return carry

    lax.fori_loop(0, head_devices // 2, pair_body, 0)

    for condition, copy in sent:
        when(condition, copy.wait_send)
    for step in range(last):
        for chunk in range(chunks):
            when(both(z >= step, z < last), norm_copy(z - step, 1, chunk).wait_send)
            when(both(z + step <= last, z > 0), norm_copy(z + step, -1, chunk).wait_send)


def per_device(query_latent, norm_gain, kv_latent, q_up, absorb_key, absorb_value, block_owner):
    head_devices = lax.axis_size("head")
    ctx_count = lax.axis_size("ctx")
    rows, query_width = query_latent.shape
    kv_width = kv_latent.shape[1]
    head_count, _, value_width = absorb_value.shape
    rope_half = (kv_width - absorb_key.shape[2]) // 2
    tok_dev = rows * head_devices
    piece_count = ctx_count * head_devices
    bits = (ctx_count // 2).bit_length() - 1
    slots = head_devices * ((ctx_count // 2) * (bits + 1) * 2 + 8)
    bf16, f32 = jnp.bfloat16, jnp.float32
    whole = pl.BlockSpec(memory_space=pltpu.VMEM)
    away = pl.BlockSpec(memory_space=pl.ANY)
    out = pl.pallas_call(
        functools.partial(kernel, ctx_count, head_devices),
        out_shape=jax.ShapeDtypeStruct((head_devices // 2, 2 * rows, head_count * value_width), bf16),
        in_specs=[pl.BlockSpec(memory_space=pltpu.SMEM)] + [away] * 6,
        out_specs=whole,
        scratch_shapes=[
            pltpu.VMEM(query_latent.shape, bf16),
            pltpu.VMEM(norm_gain.shape, bf16),
            pltpu.VMEM(q_up.shape, bf16),
            pltpu.VMEM(absorb_key.shape, bf16),
            pltpu.VMEM(absorb_value.shape, bf16),
            pltpu.VMEM((piece_count, rows, kv_width), bf16),
            pltpu.VMEM((head_devices // 2, 2 * rows, query_width), bf16),
            pltpu.VMEM((tok_dev, rope_half), f32),
            pltpu.VMEM((tok_dev, rope_half), f32),
            pltpu.VMEM((2, ctx_count * tok_dev // 2), jnp.int32),
            pltpu.VMEM((2 * rows, q_up.shape[1]), f32),
            pltpu.VMEM((2 * head_count * rows, kv_width), bf16),
            pltpu.SemaphoreType.DMA((piece_count,)),
            pltpu.SemaphoreType.DMA((slots,)),
            pltpu.SemaphoreType.DMA((2 * head_devices,)),
            pltpu.SemaphoreType.DMA((2 * head_devices,)),
            pltpu.SemaphoreType.DMA((2 * head_devices,)),
            pltpu.SemaphoreType.DMA((6,)),
        ],
        compiler_params=pltpu.CompilerParams(
            collective_id=0, has_side_effects=True, vmem_limit_bytes=60 * 1024 * 1024
        ),
    )(
        block_owner,
        query_latent,
        norm_gain,
        kv_latent,
        q_up,
        absorb_key,
        absorb_value,
    )
    return out.reshape(tok_dev, head_count * value_width)


def solution(mesh):
    return jax.shard_map(
        per_device,
        mesh=mesh,
        in_specs=(
            P(("ctx", "head"), None),
            P(),
            P(("ctx", "head"), None),
            P(None, "head"),
            P("head", None, None),
            P("head", None, None),
            P(),
        ),
        out_specs=P("ctx", "head"),
        check_vma=False,
    )
```

```python
import functools
import math

import jax
import jax.numpy as jnp
from jax import lax
from jax.experimental import pallas as pl
from jax.experimental.pallas import tpu as pltpu
from jax.sharding import PartitionSpec as P

epsilon = 1e-06
masked_score = -1e30
MESH = pl.DeviceIdType.MESH


def when(condition, action):
    if condition is True:
        action()
    else:
        pl.when(condition)(action)


def both(first, second):
    if first is True:
        return second
    if second is True:
        return first
    return jnp.logical_and(first, second)


def kernel(
    ctx_count,
    head_devices,
    owner_ref,
    query_hbm,
    gain_hbm,
    kv_hbm,
    q_up_hbm,
    absorb_key_hbm,
    absorb_value_hbm,
    out_ref,
    query_ref,
    gain_ref,
    q_up_ref,
    absorb_key_ref,
    absorb_value_ref,
    kv_all,
    normed_all,
    cosine_ref,
    sine_ref,
    key_pos_ref,
    projected_ref,
    queries_ref,
    kv_recv,
    kv_send,
    norm_recv,
    norm_send_up,
    norm_send_down,
    load_sem,
):
    rows = query_ref.shape[0]
    head_count, nope_width, latent_width = absorb_key_ref.shape
    value_width = absorb_value_ref.shape[2]
    head_width = q_up_ref.shape[1] // head_count
    rope_width = head_width - nope_width
    half_width = rope_width // 2
    tok_dev = rows * head_devices
    half_len = tok_dev // 2
    chips = ctx_count // 2
    bits = chips.bit_length() - 1
    last = head_devices - 1
    ctx = lax.axis_index("ctx")
    z = lax.axis_index("head")

    def across(relative):
        place = ctx
        for bit in range(bits):
            if (relative >> bit) & 1:
                weight = 2 ** (bit + 1)
                place = place + weight - 2 * weight * lax.rem(lax.div(ctx, weight), 2)
        return place

    def other_core(place):
        return place + 1 - 2 * lax.rem(place, 2)

    sibling = other_core(ctx)

    halves = head_devices // 2
    half_pieces = ctx_count * halves

    def slot_of(origin, piece):
        return lax.div(piece, halves) * half_pieces + origin * halves + lax.rem(piece, halves)

    loads = [
        pltpu.make_async_copy(kv_hbm, kv_all.at[slot_of(ctx, z)], load_sem.at[3]),
        pltpu.make_async_copy(query_hbm, query_ref, load_sem.at[4]),
        pltpu.make_async_copy(gain_hbm, gain_ref, load_sem.at[5]),
        pltpu.make_async_copy(q_up_hbm, q_up_ref, load_sem.at[0]),
        pltpu.make_async_copy(absorb_key_hbm, absorb_key_ref, load_sem.at[1]),
        pltpu.make_async_copy(absorb_value_hbm, absorb_value_ref, load_sem.at[2]),
    ]

    for load in loads:
        load.start()

    barrier = pltpu.get_barrier_semaphore()
    for bit in range(bits):
        pl.semaphore_signal(barrier, inc=1, device_id=(across(1 << bit), z), device_id_type=MESH)
    pl.semaphore_signal(barrier, inc=1, device_id=(sibling, z), device_id_type=MESH)

    kv_reach = min(2, last)
    partners = bits + 1
    for step in range(1, kv_reach + 1):
        for valid, place in ((z + step <= last, z + step), (z >= step, z - step)):
            partners = partners + jnp.where(valid, 1, 0)
            when(
                valid,
                functools.partial(
                    pl.semaphore_signal,
                    barrier,
                    inc=1,
                    device_id=(ctx, place),
                    device_id_type=MESH,
                ),
            )

    loads[0].wait()
    pl.semaphore_wait(barrier, partners)

    sent = []

    def kv_copy(origin, piece, slot, target):
        index = slot_of(origin, piece)
        return pltpu.make_async_remote_copy(
            src_ref=kv_all.at[index],
            dst_ref=kv_all.at[index],
            send_sem=kv_send.at[slot],
            recv_sem=kv_recv.at[index],
            device_id=target,
            device_id_type=MESH,
        )

    def send_kv(condition, origin, piece, target):
        copy = kv_copy(origin, piece, len(sent), target)
        sent.append((condition, copy))
        when(condition, copy.start)

    def wait_kv(condition, origin, piece):
        when(condition, kv_copy(origin, piece, 0, (sibling, z)).wait_recv)

    def pieces(step):
        if step == 0:
            return [(True, z, 0)]
        return [(z >= step, z - step, 1), (z + step <= last, z + step, -1)]

    def own_block(step):
        if step == 0:
            for far in range(1, kv_reach + 1):
                send_kv(z + far <= last, ctx, z, (ctx, z + far))
                send_kv(z >= far, ctx, z, (ctx, z - far))
        for valid, piece, way in pieces(step):
            if step > 0:
                wait_kv(valid, ctx, piece)
            if kv_reach <= step < last:
                onward = z < last if way > 0 else z > 0
                send_kv(both(valid, onward), ctx, piece, (ctx, z + way))
            for bit in range(bits):
                send_kv(valid, ctx, piece, (across(1 << bit), z))
            send_kv(valid, ctx, piece, (sibling, z))

    def relay(step, relative):
        origin = across(relative)
        for valid, piece, _ in pieces(step):
            wait_kv(valid, origin, piece)
            even = lax.rem(piece + head_devices, 2) == 0
            for bit in range(bits):
                if relative < (1 << bit):
                    send_kv(both(valid, even), origin, piece, (across(1 << bit), z))
                elif relative & ((2 << bit) - 1) == 0:
                    odd = jnp.logical_not(even)
                    send_kv(both(valid, odd), origin, piece, (across(1 << bit), z))
            send_kv(valid, origin, piece, (sibling, z))

    chunks = 2 if rows % 32 == 0 else 1
    chunk_rows = rows // chunks

    def norm_copy(block, way, chunk):
        send_sem = norm_send_up if way > 0 else norm_send_down
        begin = pl.multiple_of(lax.rem(block, 2) * rows + chunk * chunk_rows, chunk_rows)
        view = normed_all.at[lax.div(block, 2), pl.ds(begin, chunk_rows)]
        index = block * chunks + chunk
        return pltpu.make_async_remote_copy(
            src_ref=view,
            dst_ref=view,
            send_sem=send_sem.at[index],
            recv_sem=norm_recv.at[index],
            device_id=(ctx, z + way),
            device_id_type=MESH,
        )

    def norm_blocks(step):
        return (
            (z >= step, z - step, 1, z < last),
            (z + step <= last, z + step, -1, z > 0),
        )

    def norm_forward(step, some=range(chunks)):
        for chunk in some:
            for valid, block, way, onward in norm_blocks(step):
                copy = norm_copy(block, way, chunk)
                when(both(valid, onward), copy.wait_recv)
                when(both(valid, onward), copy.start)

    def norm_take(step):
        for chunk in range(chunks):
            for valid, block, way, onward in norm_blocks(step):
                here = jnp.logical_and(valid, jnp.logical_not(onward))
                when(here, norm_copy(block, way, chunk).wait_recv)

    own_block(0)
    loads[1].wait()
    loads[2].wait()
    query_f32 = query_ref[...].astype(jnp.float32)
    own_row = pl.multiple_of(lax.rem(z, 2) * rows, rows)
    normed_all[lax.div(z, 2), pl.ds(own_row, rows)] = (
        query_f32
        * lax.rsqrt(jnp.mean(query_f32 * query_f32, axis=-1, keepdims=True) + epsilon)
        * gain_ref[...].reshape(1, -1).astype(jnp.float32)
    ).astype(jnp.bfloat16)

    def send_norm(some):
        for chunk in some:
            when(z < last, norm_copy(z, 1, chunk).start)
            when(z > 0, norm_copy(z, -1, chunk).start)

    send_norm(range(1))

    def half_base(owner, upper):
        return jnp.where(upper, 2 * ctx_count - 1 - owner, owner) * half_len

    def tables():
        own = owner_ref[ctx]
        groups = 128 // half_width
        span = tok_dev // groups
        lanes = lax.broadcasted_iota(jnp.int32, (span, 128), 1)
        offset = lax.broadcasted_iota(jnp.int32, (span, 128), 0) + span * lax.div(
            lanes, half_width
        )
        places = jnp.where(
            offset < half_len,
            own * half_len + offset,
            (2 * ctx_count - 1 - own) * half_len + offset - half_len,
        )
        frequency = jnp.exp(
            lax.rem(lanes[:1], half_width).astype(jnp.float32)
            * (-math.log(10000.0) / half_width)
        )
        angles = places.astype(jnp.float32) * frequency
        cosine, sine = jnp.cos(angles), jnp.sin(angles)
        for group in range(groups):
            begin = group * half_width
            cosine_ref[group * span : (group + 1) * span] = cosine[:, begin : begin + half_width]
            sine_ref[group * span : (group + 1) * span] = sine[:, begin : begin + half_width]
        lane = lax.broadcasted_iota(jnp.int32, (1, half_len), 1)
        for index in range(ctx_count):
            owner = owner_ref[index]
            columns = slice(index * half_len, (index + 1) * half_len)
            key_pos_ref[:1, columns] = owner * half_len + lane
            key_pos_ref[1:, columns] = (2 * ctx_count - 1 - owner) * half_len + lane

    distances = [
        [r for r in range(chips) if bin(r).count("1") == level] for level in range(bits + 1)
    ]
    for stage in range(head_devices + bits):
        if 0 < stage < head_devices:
            own_block(stage)
        if stage == min(kv_reach, last):
            send_norm(range(1, chunks))
        for level in range(1, bits + 1):
            if 0 <= stage - level < head_devices:
                for relative in distances[level]:
                    relay(stage - level, relative)
            if stage == last + level == last + 1:
                norm_forward(1, range(1, chunks))
        if stage == 0:
            tables()
        if stage == last:
            norm_forward(1, range(1))
    norm_take(1)
    for load in loads[3:]:
        load.wait()

    factor = float(head_width) ** (-0.5) * math.log2(math.e)
    pair_rows = 2 * rows
    own_pair = lax.div(z, 2)
    last_pair = last // 2
    shorter = jnp.minimum(own_pair, last_pair - own_pair)

    def pair_at(step):
        near = own_pair + lax.div(step + 1, 2) * (1 - 2 * lax.rem(step, 2))
        far = jnp.where(own_pair > last_pair - own_pair, last_pair - step, step)
        return jnp.where(step <= 2 * shorter, near, far)

    def project(pair):
        projected_ref[...] = jnp.dot(
            normed_all[pair], q_up_ref[...], preferred_element_type=jnp.float32
        )
        cosine = cosine_ref[pl.ds(pl.multiple_of(pair * pair_rows, pair_rows), pair_rows)]
        sine = sine_ref[pl.ds(pl.multiple_of(pair * pair_rows, pair_rows), pair_rows)]
        for head in range(head_count):
            begin = head * head_width
            q_nope = projected_ref[:, begin : begin + nope_width].astype(jnp.bfloat16)
            q_abs = jnp.dot(q_nope, absorb_key_ref[head], preferred_element_type=jnp.float32)
            begin += nope_width
            front = projected_ref[:, begin : begin + half_width]
            back = projected_ref[:, begin + half_width : begin + rope_width]
            span = slice(head * pair_rows, (head + 1) * pair_rows)
            queries_ref[span, :latent_width] = q_abs.astype(jnp.bfloat16)
            queries_ref[span, latent_width:] = jnp.concatenate(
                [front * cosine - back * sine, front * sine + back * cosine], axis=-1
            ).astype(jnp.bfloat16)

    project(own_pair)
    for relative in range(chips):
        for piece in range(head_devices):
            wait_kv(True, other_core(across(relative)), piece)

    if last > 1:
        norm_forward(2, range(1))

    def pair_body(step, carry):
        pair = pair_at(step)
        offset = pair * pair_rows
        base = half_base(owner_ref[ctx], offset >= half_len) + lax.rem(offset, half_len)
        query_pos = base + lax.rem(
            lax.broadcasted_iota(jnp.int32, (head_count * pair_rows, 1), 0), pair_rows
        )

        def attend(upper):
            def rows_of(half):
                return kv_all[half * half_pieces : (half + 1) * half_pieces].reshape(
                    ctx_count * half_len, latent_width + rope_width
                )

            def score(keys):
                return lax.dot_general(
                    queries_ref[...],
                    keys,
                    (((1,), (1,)), ((), ())),
                    preferred_element_type=jnp.float32,
                )

            allowed = key_pos_ref[int(upper) : int(upper) + 1] <= query_pos
            parts = [jnp.where(allowed, score(rows_of(int(upper))), masked_score)]
            peak = jnp.max(parts[0], axis=-1, keepdims=True)
            if upper:
                parts.append(score(rows_of(0)))
                peak = jnp.maximum(peak, jnp.max(parts[1], axis=-1, keepdims=True))

            @pl.when(jnp.logical_and(step == 0, last > 1))
            def _():
                norm_forward(2, range(1, chunks))

            total, weighted = 0.0, 0.0
            for half, part in zip((int(upper), 0), parts):
                weights = jnp.exp2((part - peak) * factor)
                total += jnp.sum(weights, axis=-1, keepdims=True)
                weighted += jnp.dot(
                    weights.astype(jnp.bfloat16),
                    rows_of(half)[:, :latent_width],
                    preferred_element_type=jnp.float32,
                )
            queries_ref[:, :latent_width] = (weighted / total).astype(jnp.bfloat16)

        pl.when(2 * pair < halves)(functools.partial(attend, False))
        pl.when(2 * pair >= halves)(functools.partial(attend, True))
        for head in range(head_count):
            out_ref[pair, :, head * value_width : (head + 1) * value_width] = jnp.dot(
                queries_ref[head * pair_rows : (head + 1) * pair_rows, :latent_width],
                absorb_value_ref[head],
                preferred_element_type=jnp.float32,
            ).astype(jnp.bfloat16)

        @pl.when(step < last_pair)
        def _():
            norm_take(2 * step + 2)
            for further in (2 * step + 3, 2 * step + 4):
                norm_forward(further)
            norm_take(2 * step + 3)

            project(pair_at(step + 1))

        return carry

    lax.fori_loop(0, head_devices // 2, pair_body, 0)

    for condition, copy in sent:
        when(condition, copy.wait_send)
    for step in range(last):
        for chunk in range(chunks):
            when(both(z >= step, z < last), norm_copy(z - step, 1, chunk).wait_send)
            when(both(z + step <= last, z > 0), norm_copy(z + step, -1, chunk).wait_send)


def per_device(query_latent, norm_gain, kv_latent, q_up, absorb_key, absorb_value, block_owner):
    head_devices = lax.axis_size("head")
    ctx_count = lax.axis_size("ctx")
    rows, query_width = query_latent.shape
    kv_width = kv_latent.shape[1]
    head_count, _, value_width = absorb_value.shape
    rope_half = (kv_width - absorb_key.shape[2]) // 2
    tok_dev = rows * head_devices
    piece_count = ctx_count * head_devices
    bits = (ctx_count // 2).bit_length() - 1
    slots = head_devices * ((ctx_count // 2) * (bits + 1) * 2 + 8)
    bf16, f32 = jnp.bfloat16, jnp.float32
    whole = pl.BlockSpec(memory_space=pltpu.VMEM)
    away = pl.BlockSpec(memory_space=pl.ANY)
    out = pl.pallas_call(
        functools.partial(kernel, ctx_count, head_devices),
        out_shape=jax.ShapeDtypeStruct((head_devices // 2, 2 * rows, head_count * value_width), bf16),
        in_specs=[pl.BlockSpec(memory_space=pltpu.SMEM)] + [away] * 6,
        out_specs=whole,
        scratch_shapes=[
            pltpu.VMEM(query_latent.shape, bf16),
            pltpu.VMEM(norm_gain.shape, bf16),
            pltpu.VMEM(q_up.shape, bf16),
            pltpu.VMEM(absorb_key.shape, bf16),
            pltpu.VMEM(absorb_value.shape, bf16),
            pltpu.VMEM((piece_count, rows, kv_width), bf16),
            pltpu.VMEM((head_devices // 2, 2 * rows, query_width), bf16),
            pltpu.VMEM((tok_dev, rope_half), f32),
            pltpu.VMEM((tok_dev, rope_half), f32),
            pltpu.VMEM((2, ctx_count * tok_dev // 2), jnp.int32),
            pltpu.VMEM((2 * rows, q_up.shape[1]), f32),
            pltpu.VMEM((2 * head_count * rows, kv_width), bf16),
            pltpu.SemaphoreType.DMA((piece_count,)),
            pltpu.SemaphoreType.DMA((slots,)),
            pltpu.SemaphoreType.DMA((2 * head_devices,)),
            pltpu.SemaphoreType.DMA((2 * head_devices,)),
            pltpu.SemaphoreType.DMA((2 * head_devices,)),
            pltpu.SemaphoreType.DMA((6,)),
        ],
        compiler_params=pltpu.CompilerParams(
            collective_id=0, has_side_effects=True, vmem_limit_bytes=60 * 1024 * 1024
        ),
    )(
        block_owner,
        query_latent,
        norm_gain,
        kv_latent,
        q_up,
        absorb_key,
        absorb_value,
    )
    return out.reshape(tok_dev, head_count * value_width)


def solution(mesh):
    return jax.shard_map(
        per_device,
        mesh=mesh,
        in_specs=(
            P(("ctx", "head"), None),
            P(),
            P(("ctx", "head"), None),
            P(None, "head"),
            P("head", None, None),
            P("head", None, None),
            P(),
        ),
        out_specs=P("ctx", "head"),
        check_vma=False,
    )
```

```python
import functools
import math

import jax
import jax.numpy as jnp
from jax import lax
from jax.experimental import pallas as pl
from jax.experimental.pallas import tpu as pltpu
from jax.sharding import PartitionSpec as P

epsilon = 1e-06
masked_score = -1e30
MESH = pl.DeviceIdType.MESH


def when(condition, action):
    if condition is True:
        action()
    else:
        pl.when(condition)(action)


def both(first, second):
    if first is True:
        return second
    if second is True:
        return first
    return jnp.logical_and(first, second)


def kernel(
    ctx_count,
    head_devices,
    owner_ref,
    query_hbm,
    gain_hbm,
    kv_hbm,
    q_up_hbm,
    absorb_key_hbm,
    absorb_value_hbm,
    out_ref,
    query_ref,
    gain_ref,
    q_up_ref,
    absorb_key_ref,
    absorb_value_ref,
    kv_all,
    normed_all,
    cosine_ref,
    sine_ref,
    key_pos_ref,
    projected_ref,
    queries_ref,
    kv_recv,
    kv_send,
    norm_recv,
    norm_send_up,
    norm_send_down,
    load_sem,
):
    rows = query_ref.shape[0]
    head_count, nope_width, latent_width = absorb_key_ref.shape
    value_width = absorb_value_ref.shape[2]
    head_width = q_up_ref.shape[1] // head_count
    rope_width = head_width - nope_width
    half_width = rope_width // 2
    tok_dev = rows * head_devices
    half_len = tok_dev // 2
    chips = ctx_count // 2
    bits = chips.bit_length() - 1
    last = head_devices - 1
    ctx = lax.axis_index("ctx")
    z = lax.axis_index("head")

    def across(relative):
        place = ctx
        for bit in range(bits):
            if (relative >> bit) & 1:
                weight = 2 ** (bit + 1)
                place = place + weight - 2 * weight * lax.rem(lax.div(ctx, weight), 2)
        return place

    def other_core(place):
        return place + 1 - 2 * lax.rem(place, 2)

    sibling = other_core(ctx)

    halves = head_devices // 2
    half_pieces = ctx_count * halves

    def slot_of(origin, piece):
        return lax.div(piece, halves) * half_pieces + origin * halves + lax.rem(piece, halves)

    loads = [
        pltpu.make_async_copy(kv_hbm, kv_all.at[slot_of(ctx, z)], load_sem.at[3]),
        pltpu.make_async_copy(query_hbm, query_ref, load_sem.at[4]),
        pltpu.make_async_copy(gain_hbm, gain_ref, load_sem.at[5]),
        pltpu.make_async_copy(q_up_hbm, q_up_ref, load_sem.at[0]),
        pltpu.make_async_copy(absorb_key_hbm, absorb_key_ref, load_sem.at[1]),
        pltpu.make_async_copy(absorb_value_hbm, absorb_value_ref, load_sem.at[2]),
    ]

    for load in loads:
        load.start()

    barrier = pltpu.get_barrier_semaphore()
    for bit in range(bits):
        pl.semaphore_signal(barrier, inc=1, device_id=(across(1 << bit), z), device_id_type=MESH)
    pl.semaphore_signal(barrier, inc=1, device_id=(sibling, z), device_id_type=MESH)

    kv_reach = min(2, last)
    partners = bits + 1
    for step in range(1, kv_reach + 1):
        for valid, place in ((z + step <= last, z + step), (z >= step, z - step)):
            partners = partners + jnp.where(valid, 1, 0)
            when(
                valid,
                functools.partial(
                    pl.semaphore_signal,
                    barrier,
                    inc=1,
                    device_id=(ctx, place),
                    device_id_type=MESH,
                ),
            )

    loads[0].wait()
    pl.semaphore_wait(barrier, partners)

    sent = []

    def kv_copy(origin, piece, slot, target):
        index = slot_of(origin, piece)
        return pltpu.make_async_remote_copy(
            src_ref=kv_all.at[index],
            dst_ref=kv_all.at[index],
            send_sem=kv_send.at[slot],
            recv_sem=kv_recv.at[index],
            device_id=target,
            device_id_type=MESH,
        )

    def send_kv(condition, origin, piece, target):
        copy = kv_copy(origin, piece, len(sent), target)
        sent.append((condition, copy))
        when(condition, copy.start)

    def wait_kv(condition, origin, piece):
        when(condition, kv_copy(origin, piece, 0, (sibling, z)).wait_recv)

    def pieces(step):
        if step == 0:
            return [(True, z, 0)]
        return [(z >= step, z - step, 1), (z + step <= last, z + step, -1)]

    def own_block(step):
        if step == 0:
            for far in range(1, kv_reach + 1):
                send_kv(z + far <= last, ctx, z, (ctx, z + far))
                send_kv(z >= far, ctx, z, (ctx, z - far))
        for valid, piece, way in pieces(step):
            if step > 0:
                wait_kv(valid, ctx, piece)
            if kv_reach <= step < last:
                onward = z < last if way > 0 else z > 0
                send_kv(both(valid, onward), ctx, piece, (ctx, z + way))
            for bit in range(bits):
                send_kv(valid, ctx, piece, (across(1 << bit), z))
            send_kv(valid, ctx, piece, (sibling, z))

    def relay(step, relative):
        origin = across(relative)
        for valid, piece, _ in pieces(step):
            wait_kv(valid, origin, piece)
            even = lax.rem(piece + head_devices, 2) == 0
            for bit in range(bits):
                if relative < (1 << bit):
                    send_kv(both(valid, even), origin, piece, (across(1 << bit), z))
                elif relative & ((2 << bit) - 1) == 0:
                    odd = jnp.logical_not(even)
                    send_kv(both(valid, odd), origin, piece, (across(1 << bit), z))
            send_kv(valid, origin, piece, (sibling, z))

    chunks = 2 if rows % 32 == 0 else 1
    chunk_rows = rows // chunks

    def norm_copy(block, way, chunk):
        send_sem = norm_send_up if way > 0 else norm_send_down
        begin = pl.multiple_of(lax.rem(block, 2) * rows + chunk * chunk_rows, chunk_rows)
        view = normed_all.at[lax.div(block, 2), pl.ds(begin, chunk_rows)]
        index = block * chunks + chunk
        return pltpu.make_async_remote_copy(
            src_ref=view,
            dst_ref=view,
            send_sem=send_sem.at[index],
            recv_sem=norm_recv.at[index],
            device_id=(ctx, z + way),
            device_id_type=MESH,
        )

    def norm_blocks(step):
        return (
            (z >= step, z - step, 1, z < last),
            (z + step <= last, z + step, -1, z > 0),
        )

    def norm_forward(step, some=range(chunks)):
        for chunk in some:
            for valid, block, way, onward in norm_blocks(step):
                copy = norm_copy(block, way, chunk)
                when(both(valid, onward), copy.wait_recv)
                when(both(valid, onward), copy.start)

    def norm_take(step):
        for chunk in range(chunks):
            for valid, block, way, onward in norm_blocks(step):
                here = jnp.logical_and(valid, jnp.logical_not(onward))
                when(here, norm_copy(block, way, chunk).wait_recv)

    own_block(0)
    loads[1].wait()
    loads[2].wait()
    query_f32 = query_ref[...].astype(jnp.float32)
    own_row = pl.multiple_of(lax.rem(z, 2) * rows, rows)
    normed_all[lax.div(z, 2), pl.ds(own_row, rows)] = (
        query_f32
        * lax.rsqrt(jnp.mean(query_f32 * query_f32, axis=-1, keepdims=True) + epsilon)
        * gain_ref[...].reshape(1, -1).astype(jnp.float32)
    ).astype(jnp.bfloat16)

    def send_norm(some):
        for chunk in some:
            when(z < last, norm_copy(z, 1, chunk).start)
            when(z > 0, norm_copy(z, -1, chunk).start)

    send_norm(range(1))

    def half_base(owner, upper):
        return jnp.where(upper, 2 * ctx_count - 1 - owner, owner) * half_len

    def tables():
        own = owner_ref[ctx]
        groups = 128 // half_width
        span = tok_dev // groups
        lanes = lax.broadcasted_iota(jnp.int32, (span, 128), 1)
        offset = lax.broadcasted_iota(jnp.int32, (span, 128), 0) + span * lax.div(
            lanes, half_width
        )
        places = jnp.where(
            offset < half_len,
            own * half_len + offset,
            (2 * ctx_count - 1 - own) * half_len + offset - half_len,
        )
        frequency = jnp.exp(
            lax.rem(lanes[:1], half_width).astype(jnp.float32)
            * (-math.log(10000.0) / half_width)
        )
        angles = places.astype(jnp.float32) * frequency
        cosine, sine = jnp.cos(angles), jnp.sin(angles)
        for group in range(groups):
            begin = group * half_width
            cosine_ref[group * span : (group + 1) * span] = cosine[:, begin : begin + half_width]
            sine_ref[group * span : (group + 1) * span] = sine[:, begin : begin + half_width]
        lane = lax.broadcasted_iota(jnp.int32, (1, half_len), 1)
        for index in range(ctx_count):
            owner = owner_ref[index]
            columns = slice(index * half_len, (index + 1) * half_len)
            key_pos_ref[:1, columns] = owner * half_len + lane
            key_pos_ref[1:, columns] = (2 * ctx_count - 1 - owner) * half_len + lane

    distances = [
        [r for r in range(chips) if bin(r).count("1") == level] for level in range(bits + 1)
    ]
    for stage in range(head_devices + bits):
        if 0 < stage < head_devices:
            own_block(stage)
        if stage == min(kv_reach, last):
            send_norm(range(1, chunks))
        if stage == last:
            norm_forward(1, range(1))
        for level in range(1, bits + 1):
            if 0 <= stage - level < head_devices:
                for relative in distances[level]:
                    relay(stage - level, relative)
            if stage == last + level == last + 1:
                norm_forward(1, range(1, chunks))
        if stage == 0:
            tables()
    norm_take(1)
    for load in loads[3:]:
        load.wait()

    factor = float(head_width) ** (-0.5) * math.log2(math.e)
    pair_rows = 2 * rows
    own_pair = lax.div(z, 2)
    last_pair = last // 2
    shorter = jnp.minimum(own_pair, last_pair - own_pair)

    def pair_at(step):
        near = own_pair + lax.div(step + 1, 2) * (1 - 2 * lax.rem(step, 2))
        far = jnp.where(own_pair > last_pair - own_pair, last_pair - step, step)
        return jnp.where(step <= 2 * shorter, near, far)

    def project(pair):
        projected_ref[...] = jnp.dot(
            normed_all[pair], q_up_ref[...], preferred_element_type=jnp.float32
        )
        cosine = cosine_ref[pl.ds(pl.multiple_of(pair * pair_rows, pair_rows), pair_rows)]
        sine = sine_ref[pl.ds(pl.multiple_of(pair * pair_rows, pair_rows), pair_rows)]
        for head in range(head_count):
            begin = head * head_width
            q_nope = projected_ref[:, begin : begin + nope_width].astype(jnp.bfloat16)
            q_abs = jnp.dot(q_nope, absorb_key_ref[head], preferred_element_type=jnp.float32)
            begin += nope_width
            front = projected_ref[:, begin : begin + half_width]
            back = projected_ref[:, begin + half_width : begin + rope_width]
            span = slice(head * pair_rows, (head + 1) * pair_rows)
            queries_ref[span, :latent_width] = q_abs.astype(jnp.bfloat16)
            queries_ref[span, latent_width:] = jnp.concatenate(
                [front * cosine - back * sine, front * sine + back * cosine], axis=-1
            ).astype(jnp.bfloat16)

    project(own_pair)
    for relative in range(chips):
        for piece in range(head_devices):
            wait_kv(True, other_core(across(relative)), piece)

    if last > 1:
        norm_forward(2, range(1))

    def pair_body(step, carry):
        pair = pair_at(step)
        offset = pair * pair_rows
        base = half_base(owner_ref[ctx], offset >= half_len) + lax.rem(offset, half_len)
        query_pos = base + lax.rem(
            lax.broadcasted_iota(jnp.int32, (head_count * pair_rows, 1), 0), pair_rows
        )

        def attend(upper):
            def rows_of(half):
                return kv_all[half * half_pieces : (half + 1) * half_pieces].reshape(
                    ctx_count * half_len, latent_width + rope_width
                )

            def score(keys):
                return lax.dot_general(
                    queries_ref[...],
                    keys,
                    (((1,), (1,)), ((), ())),
                    preferred_element_type=jnp.float32,
                )

            allowed = key_pos_ref[int(upper) : int(upper) + 1] <= query_pos
            parts = [jnp.where(allowed, score(rows_of(int(upper))), masked_score)]
            peak = jnp.max(parts[0], axis=-1, keepdims=True)
            if upper:
                parts.append(score(rows_of(0)))
                peak = jnp.maximum(peak, jnp.max(parts[1], axis=-1, keepdims=True))

            @pl.when(jnp.logical_and(step == 0, last > 1))
            def _():
                norm_forward(2, range(1, chunks))

            total, weighted = 0.0, 0.0
            for half, part in zip((int(upper), 0), parts):
                weights = jnp.exp2((part - peak) * factor)
                total += jnp.sum(weights, axis=-1, keepdims=True)
                weighted += jnp.dot(
                    weights.astype(jnp.bfloat16),
                    rows_of(half)[:, :latent_width],
                    preferred_element_type=jnp.float32,
                )
            queries_ref[:, :latent_width] = (weighted / total).astype(jnp.bfloat16)

        pl.when(2 * pair < halves)(functools.partial(attend, False))
        pl.when(2 * pair >= halves)(functools.partial(attend, True))
        for head in range(head_count):
            out_ref[pair, :, head * value_width : (head + 1) * value_width] = jnp.dot(
                queries_ref[head * pair_rows : (head + 1) * pair_rows, :latent_width],
                absorb_value_ref[head],
                preferred_element_type=jnp.float32,
            ).astype(jnp.bfloat16)

        @pl.when(step < last_pair)
        def _():
            norm_take(2 * step + 2)
            for further in (2 * step + 3, 2 * step + 4):
                norm_forward(further)
            norm_take(2 * step + 3)

            project(pair_at(step + 1))

        return carry

    lax.fori_loop(0, head_devices // 2, pair_body, 0)

    for condition, copy in sent:
        when(condition, copy.wait_send)
    for step in range(last):
        for chunk in range(chunks):
            when(both(z >= step, z < last), norm_copy(z - step, 1, chunk).wait_send)
            when(both(z + step <= last, z > 0), norm_copy(z + step, -1, chunk).wait_send)


def per_device(query_latent, norm_gain, kv_latent, q_up, absorb_key, absorb_value, block_owner):
    head_devices = lax.axis_size("head")
    ctx_count = lax.axis_size("ctx")
    rows, query_width = query_latent.shape
    kv_width = kv_latent.shape[1]
    head_count, _, value_width = absorb_value.shape
    rope_half = (kv_width - absorb_key.shape[2]) // 2
    tok_dev = rows * head_devices
    piece_count = ctx_count * head_devices
    bits = (ctx_count // 2).bit_length() - 1
    slots = head_devices * ((ctx_count // 2) * (bits + 1) * 2 + 8)
    bf16, f32 = jnp.bfloat16, jnp.float32
    whole = pl.BlockSpec(memory_space=pltpu.VMEM)
    away = pl.BlockSpec(memory_space=pl.ANY)
    out = pl.pallas_call(
        functools.partial(kernel, ctx_count, head_devices),
        out_shape=jax.ShapeDtypeStruct((head_devices // 2, 2 * rows, head_count * value_width), bf16),
        in_specs=[pl.BlockSpec(memory_space=pltpu.SMEM)] + [away] * 6,
        out_specs=whole,
        scratch_shapes=[
            pltpu.VMEM(query_latent.shape, bf16),
            pltpu.VMEM(norm_gain.shape, bf16),
            pltpu.VMEM(q_up.shape, bf16),
            pltpu.VMEM(absorb_key.shape, bf16),
            pltpu.VMEM(absorb_value.shape, bf16),
            pltpu.VMEM((piece_count, rows, kv_width), bf16),
            pltpu.VMEM((head_devices // 2, 2 * rows, query_width), bf16),
            pltpu.VMEM((tok_dev, rope_half), f32),
            pltpu.VMEM((tok_dev, rope_half), f32),
            pltpu.VMEM((2, ctx_count * tok_dev // 2), jnp.int32),
            pltpu.VMEM((2 * rows, q_up.shape[1]), f32),
            pltpu.VMEM((2 * head_count * rows, kv_width), bf16),
            pltpu.SemaphoreType.DMA((piece_count,)),
            pltpu.SemaphoreType.DMA((slots,)),
            pltpu.SemaphoreType.DMA((2 * head_devices,)),
            pltpu.SemaphoreType.DMA((2 * head_devices,)),
            pltpu.SemaphoreType.DMA((2 * head_devices,)),
            pltpu.SemaphoreType.DMA((6,)),
        ],
        compiler_params=pltpu.CompilerParams(
            collective_id=0, has_side_effects=True, vmem_limit_bytes=60 * 1024 * 1024
        ),
    )(
        block_owner,
        query_latent,
        norm_gain,
        kv_latent,
        q_up,
        absorb_key,
        absorb_value,
    )
    return out.reshape(tok_dev, head_count * value_width)


def solution(mesh):
    return jax.shard_map(
        per_device,
        mesh=mesh,
        in_specs=(
            P(("ctx", "head"), None),
            P(),
            P(("ctx", "head"), None),
            P(None, "head"),
            P("head", None, None),
            P("head", None, None),
            P(),
        ),
        out_specs=P("ctx", "head"),
        check_vma=False,
    )
```
